32 devices in a mesh: rows: 8 (over z, core), cols: 4 (over y, x).
Axes of the slice: x: 2, y: 2, z: 4, core: 2. Of those that a mesh axis runs over, the one named last changes fastest.
Arguments:
- item_factors: bfloat16 [128, 16384], P('cols', 'rows'), may hold values from -0.5 to 0.5
- send_list: int32 [8, 8, 32], P('rows'), may hold values from 0 to 2047, as said below
- obs_slot: int32 [64, 8192], P(None, 'rows'), may hold values from 0 to 255, as said below
- obs_weight: float32 [64, 8192], P(None, 'rows'), may hold values from 0.1 to 10
- rating: float32 [64, 8192], P(None, 'rows'), may hold values from -6 to 6
- counts: int32 [8192], P('rows'), may hold values from 5 to 64, as said below
Outputs:
- user_factors: float32 [128, 8192], P('cols', 'rows')
The draws below stay inside these ranges and needn't reach their ends.
Inputs may be any that keep to these rules, and one draw needn't show every extreme that they name: `send_list`: for each source and destination block the 32 indices are distinct. `obs_slot`: the live slots of one user name distinct positions. `counts`: in every draw some user has 64 live slots.
All inputs are finite; a program needn't handle non-finite values.
Results may differ from the reference program's by a relative error of at most 0.0007.
Values may be sent and summed in bfloat16 or wider, within the bound.
No kernel may reach another device: no remote copies, remote signals or barrier semaphores. Data moves between devices by JAX's collectives and lax.ppermute only.
A program may use at most 64 MiB of HBM per device.

```python
import math
import jax
import jax.numpy as jnp
from jax import lax

K = 128
U_DEV = 1024
I_DEV = 2048
OBS = 64
SLOTS = 32
ITERS = 4
USERS = 8192
ITEMS = 16384
N_ROWS = 8


def shared_counts(key):
    key_caps, key_rest = jax.random.split(jax.random.fold_in(key, 11))
    floor_count = ITERS + 1
    low_cap = max(OBS // 2, floor_count + 1)
    block_caps = jax.random.randint(key_caps, (N_ROWS,), low_cap, OBS + 1)
    block_caps = block_caps.at[0].set(OBS)
    draws = jax.random.randint(key_rest, (N_ROWS, U_DEV), 0, 1 << 20)
    result = floor_count + draws % (block_caps[:, None] - floor_count + 1)
    result = result.at[:, 0].set(block_caps)
    return result.reshape(USERS).astype(jnp.int32)


def draw_counts(key, part):
    return shared_counts(key)


def draw_send_list(key, part):
    key = jax.random.fold_in(key, 5)
    scores = jax.random.randint(key, (N_ROWS, N_ROWS, I_DEV), 0, 1 << 20)
    scores = scores * I_DEV + jnp.arange(I_DEV, dtype=jnp.int32)[None, None, :]
    chosen = jnp.argsort(scores, axis=-1, stable=True)[:, :, :SLOTS]
    return chosen.astype(jnp.int32)


def draw_obs_slot(key, part):
    live = shared_counts(key)
    key = jax.random.fold_in(key, 7)
    key_live, key_dead = jax.random.split(key)
    total = N_ROWS * SLOTS
    scores = jax.random.randint(key_live, (USERS, total), 0, 1 << 20)
    scores = scores * total + jnp.arange(total, dtype=jnp.int32)[None, :]
    distinct = jnp.argsort(scores, axis=-1, stable=True)[:, :OBS].astype(jnp.int32)
    dead = jax.random.randint(key_dead, (USERS, OBS), 0, total)
    position = jnp.arange(OBS, dtype=jnp.int32)[None, :]
    result = jnp.where(position < live[:, None], distinct, dead)
    return jnp.transpose(result).astype(jnp.int32)


def block_levels(own_key, extent, cuts, least, top_value):
    loudness, own = 1.0, jax.random.fold_in(own_key, 6)
    for axis_at, shards_of in cuts:
        heights = jnp.exp(jax.random.uniform(jax.random.fold_in(own, axis_at), (shards_of,), jnp.float32, least / len(cuts), top_value / len(cuts)))
        loudness = loudness * jnp.repeat(heights, extent[axis_at] // shards_of).reshape([-1 if axis == axis_at else 1 for axis in range(len(extent))])
    return loudness


def noise(own_key, dims, width, most, cuts=(), kind=jnp.bfloat16):
    loudness = block_levels(own_key, dims, cuts, -0.22, 0.18) if cuts else 1.0
    array = jax.random.normal(own_key, dims, jnp.float32) * width * loudness
    return jnp.minimum(jnp.maximum(array, -most), most).astype(kind)


def setup_inputs(seed: int = 0) -> dict:
    keys = jax.random.split(jax.random.key(seed), 7)
    return {
        "item_factors": noise(keys[0], (K, ITEMS), K ** -0.5, 0.5, ((0, 4), (1, 8))),
        "send_list": draw_send_list(jax.random.fold_in(keys[6], 71), 0),
        "obs_slot": draw_obs_slot(jax.random.fold_in(keys[6], 71), 0),
        "obs_weight": jnp.clip(jnp.exp(math.log(10.0) - 4.6051702 * jax.random.uniform(keys[3], (OBS, USERS), jnp.float32) ** block_levels(keys[3], (OBS, USERS), ((1, 8),), -0.2, 0.2)), 0.1, 10.0),
        "rating": noise(keys[4], (OBS, USERS), 1.0, 6.0, ((1, 8),), jnp.float32),
        "counts": draw_counts(jax.random.fold_in(keys[6], 71), 0),
    }


ridge_scale = 0.05


def conjugate(tiles, weighted, rating, ridge):
    target = jnp.sum(tiles * (weighted * rating)[None], axis=1)
    solution = jnp.zeros_like(target)
    residual = target
    direction = target
    norm_now = jnp.sum(target * target, axis=0)
    for iteration in range(ITERS):
        along = jnp.sum(tiles * direction[:, None, :], axis=0)
        scaled = weighted * along
        image = jnp.sum(tiles * scaled[None], axis=1) + ridge * direction
        curvature = jnp.sum(scaled * along, axis=0) + ridge * jnp.sum(direction * direction, axis=0)
        step_size = norm_now / curvature
        solution = solution + step_size * direction
        residual = residual - step_size * image
        norm_next = jnp.sum(residual * residual, axis=0)
        direction = residual + (norm_next / norm_now) * direction
        norm_now = norm_next
    return solution


def reference(item_factors, send_list, obs_slot, obs_weight, rating, counts):
    def solve_block(block):
        offset = block * U_DEV
        slots = lax.dynamic_slice_in_dim(obs_slot, offset, U_DEV, 1)
        source = slots // SLOTS
        within = slots % SLOTS
        local_index = send_list[source, block, within]
        item_ids = (source * I_DEV + local_index).astype(jnp.int32)
        tiles = jnp.take(item_factors, item_ids, axis=1)
        weights = lax.dynamic_slice_in_dim(obs_weight, offset, U_DEV, 1)
        values = lax.dynamic_slice_in_dim(rating, offset, U_DEV, 1)
        live = lax.dynamic_slice_in_dim(counts, offset, U_DEV, 0)
        present = jnp.arange(OBS, dtype=jnp.int32)[:, None] < live[None, :]
        weighted = jnp.where(present, weights, jnp.float32(0.0))
        ridge = ridge_scale * live.astype(jnp.float32)
        return conjugate(tiles, weighted, values, ridge)

    blocks = lax.map(solve_block, jnp.arange(N_ROWS, dtype=jnp.int32))
    return jnp.transpose(blocks, (1, 0, 2)).reshape(K, USERS)
```

```python
import functools

import jax
import jax.numpy as jnp
from jax import lax
from jax.experimental import pallas as pl
from jax.experimental.pallas import tpu as pltpu
from jax.sharding import PartitionSpec as P

ITERS = 4


ridge_scale = 0.05


def update(tiles, weighted, ridge, direction, along, length_sq, norm_now, solution, residual):
    scaled = weighted * along
    image = jnp.sum(tiles * scaled[None], axis=1) + ridge * direction
    curvature = jnp.sum(scaled * along, axis=0) + ridge * length_sq
    step_size = norm_now / curvature
    return (solution + step_size * direction, residual - step_size * image)


def squared_norm(values):
    partial_sum = jnp.sum(values * values, axis=0)
    return lax.psum(partial_sum, "cols")


def conjugate_plain(tiles, weighted, rating, ridge):
    target = jnp.sum(tiles * (weighted * rating)[None], axis=1)
    solution = jnp.zeros_like(target)
    residual = target
    direction = target
    norm_now = squared_norm(target)
    for iteration in range(ITERS):
        along_part = jnp.sum(tiles * direction[:, None, :], axis=0)
        length_part = jnp.sum(direction * direction, axis=0)
        along, length_sq = lax.psum((along_part, length_part), "cols")
        solution, residual = update(
            tiles, weighted, ridge, direction, along, length_sq, norm_now, solution, residual
        )
        if iteration + 1 < ITERS:
            norm_next = squared_norm(residual)
            direction = residual + norm_next / norm_now * direction
            norm_now = norm_next
    return solution


def sparse_shards(item_factors, send_list, obs_slot, obs_weight, rating, counts):
    columns = item_factors.shape[0]
    row_count = lax.axis_size("rows")
    slot_count = send_list.shape[2]
    outgoing = jnp.take(item_factors, send_list.reshape(-1), axis=1).reshape(
        columns, row_count, slot_count
    )
    arrived = lax.all_to_all(outgoing, "rows", split_axis=1, concat_axis=1, tiled=True).reshape(
        columns, row_count * slot_count
    )
    tiles = jnp.take(arrived, obs_slot, axis=1)
    present = jnp.arange(obs_slot.shape[0], dtype=jnp.int32)[:, None] < counts[None, :]
    weighted = jnp.where(present, obs_weight, jnp.float32(0.0))
    ridge = ridge_scale * counts.astype(jnp.float32)
    return conjugate_plain(tiles, weighted, rating, ridge)


def pieces_of(values, count):
    pieces = []
    for _ in range(count):
        piece = values.astype(jnp.bfloat16)
        pieces.append(piece)
        values = values - piece.astype(jnp.float32)
    return jnp.concatenate(pieces, axis=0)


def pick_kernel(col_count, factors_ref, list_ref, out_ref):
    factor_count, items = factors_ref.shape
    _, row_count, slots = list_ref.shape
    wanted = jnp.concatenate([list_ref[0, d : d + 1, :] for d in range(row_count)], axis=1)
    item = lax.broadcasted_iota(jnp.int32, (items, row_count * slots), 0)
    chosen = (item == wanted).astype(jnp.bfloat16)
    picked = jnp.dot(factors_ref[...], chosen, preferred_element_type=jnp.float32)
    group = lax.broadcasted_iota(jnp.int32, (8, 128), 1) // slots
    for d in range(row_count):
        start = d * slots
        base = start // 128 * 128
        chunk = jnp.zeros((8, 128), jnp.float32)
        for i in range(factor_count // 8):
            piece = picked[8 * i : 8 * i + 8, base : base + 128]
            shift = (slots * i - (start - base)) % 128
            if shift:
                piece = pltpu.roll(piece, shift, 1)
            chunk = jnp.where(group == i, piece, chunk)
        chunk = chunk.astype(jnp.bfloat16)
        for c in range(col_count):
            out_ref[d * col_count + c] = chunk


def spread_kernel(slot_ref, weight_ref, rating_ref, counts_ref, w_ref, b_ref, live_slot):
    obs, users = slot_ref.shape
    positions = w_ref.shape[0]
    rows = min(128, positions)
    order = lax.broadcasted_iota(jnp.int32, (obs, users), 0)
    live_slot[...] = jnp.where(order < counts_ref[...], slot_ref[...], -1)
    place = lax.broadcasted_iota(jnp.int32, (rows, users), 0)

    @pl.loop(0, positions // rows)
    def _(part):
        start = pl.multiple_of(part * rows, rows)
        weight = jnp.zeros((rows, users), jnp.float32)
        value = jnp.zeros((rows, users), jnp.float32)
        for o in range(obs):
            here = place == live_slot[o : o + 1, :] - start
            weight = jnp.where(here, weight_ref[o : o + 1, :], weight)
            value = jnp.where(here, rating_ref[o : o + 1, :], value)
        w_ref[pl.ds(start, rows), :] = weight
        b_ref[pl.ds(start, rows), :] = weight * value


def solve_kernel(arrived_ref, w_ref, b_ref, counts_ref, out_ref, twice_t, thrice, slots, col_count):
    own, users = out_ref.shape
    positions = w_ref.shape[0]
    factor_count = own * col_count
    row_count = positions // slots

    @pl.when(pl.program_id(0) == 0)
    def _():
        me = lax.axis_index("cols")
        group = lax.broadcasted_iota(jnp.int32, (8, 128), 1) // slots
        per_tile = 128 // slots
        for j in range(col_count):
            source = lax.rem(me + j, col_count)
            chunks = [arrived_ref[s * col_count + source].astype(jnp.float32) for s in range(row_count)]
            lines = []
            for i in range(own // 8):
                tiles = []
                for first in range(0, row_count, per_tile):
                    tile = None
                    for at in range(per_tile):
                        piece = chunks[first + at]
                        shift = (slots * (at - i)) % 128
                        if shift:
                            piece = pltpu.roll(piece, shift, 1)
                        tile = piece if tile is None else jnp.where(group == at, piece, tile)
                    tiles.append(tile)
                lines.append(jnp.concatenate(tiles, axis=1))
            block = jnp.concatenate(lines, axis=0)
            for copy in range(3):
                thrice[own * j : own * (j + 1), positions * copy : positions * (copy + 1)] = block.astype(jnp.bfloat16)
        columns_t = jnp.transpose(thrice[:, :positions].astype(jnp.float32)).astype(jnp.bfloat16)
        for copy in range(2):
            twice_t[:, factor_count * copy : factor_count * (copy + 1)] = columns_t

    def dot(left, right):
        return jnp.dot(left, right, preferred_element_type=jnp.float32)

    def total(values):
        return jnp.sum(values, axis=0, keepdims=True)

    ridge = ridge_scale * counts_ref[...].astype(jnp.float32)
    residual = dot(thrice[...], pieces_of(b_ref[...], 3))
    direction = residual
    norm_now = total(residual * residual)
    result = jnp.zeros((own, users), jnp.float32)
    for iteration in range(ITERS):
        along = dot(twice_t[...], pieces_of(direction, 2))
        scaled = w_ref[...] * along
        curvature = total(scaled * along) + ridge * total(direction * direction)
        step_size = norm_now / curvature
        result = result + step_size * direction[:own]
        if iteration + 1 < ITERS:
            image = dot(thrice[...], pieces_of(scaled, 3)) + ridge * direction
            residual = residual - step_size * image
            norm_next = total(residual * residual)
            direction = residual + norm_next / norm_now * direction
            norm_now = norm_next
    out_ref[...] = result


def dense_shards(item_factors, send_list, obs_slot, obs_weight, rating, counts):
    own, items = item_factors.shape
    row_count = lax.axis_size("rows")
    col_count = lax.axis_size("cols")
    slots = send_list.shape[2]
    obs, users = obs_slot.shape
    positions = row_count * slots
    factor_count = own * col_count
    outgoing = pl.pallas_call(
        functools.partial(pick_kernel, col_count),
        out_shape=jax.ShapeDtypeStruct((row_count * col_count, 8, 128), jnp.bfloat16),
        name="pick",
    )(item_factors, send_list)
    arrived = lax.all_to_all(outgoing, ("rows", "cols"), split_axis=0, concat_axis=0, tiled=True)
    counts = counts.reshape(1, users)
    wide = 128
    by_position = jax.ShapeDtypeStruct((positions, users), jnp.float32)
    weight, value = pl.pallas_call(
        spread_kernel,
        out_shape=(by_position, by_position),
        grid=(users // wide,),
        in_specs=[pl.BlockSpec((obs, wide), lambda u: (0, u))] * 3 + [pl.BlockSpec((1, wide), lambda u: (0, u))],
        out_specs=[pl.BlockSpec((positions, wide), lambda u: (0, u))] * 2,
        scratch_shapes=[pltpu.VMEM((obs, wide), jnp.int32)],
        cost_estimate=pl.CostEstimate(
            flops=3 * obs * positions * users, bytes_accessed=(12 * obs + 8 * positions) * users, transcendentals=0
        ),
        name="spread",
    )(obs_slot, obs_weight, rating, counts)
    wide = 256
    return pl.pallas_call(
        functools.partial(solve_kernel, slots=slots, col_count=col_count),
        out_shape=jax.ShapeDtypeStruct((own, users), jnp.float32),
        grid=(users // wide,),
        in_specs=[
            pl.BlockSpec(arrived.shape, lambda u: (0, 0, 0)),
            pl.BlockSpec((positions, wide), lambda u: (0, u)),
            pl.BlockSpec((positions, wide), lambda u: (0, u)),
            pl.BlockSpec((1, wide), lambda u: (0, u)),
        ],
        out_specs=pl.BlockSpec((own, wide), lambda u: (0, u)),
        scratch_shapes=[
            pltpu.VMEM((positions, 2 * factor_count), jnp.bfloat16),
            pltpu.VMEM((factor_count, 3 * positions), jnp.bfloat16),
        ],
        compiler_params=pltpu.CompilerParams(vmem_limit_bytes=32 << 20),
        name="solve",
    )(arrived, weight, value, counts)


def shards(item_factors, send_list, obs_slot, obs_weight, rating, counts):
    positions = lax.axis_size("rows") * send_list.shape[2]
    dense = positions <= 512 and 128 % send_list.shape[2] == 0
    work = dense_shards if dense else sparse_shards
    return work(item_factors, send_list, obs_slot, obs_weight, rating, counts)


def solution(mesh):
    placed = (
        P("cols", "rows"),
        P("rows", None, None),
        P(None, "rows"),
        P(None, "rows"),
        P(None, "rows"),
        P("rows"),
    )
    return jax.shard_map(
        shards, mesh=mesh, in_specs=placed, out_specs=P("cols", "rows"), check_vma=False
    )
```

```python
import functools

import jax
import jax.numpy as jnp
from jax import lax
from jax.experimental import pallas as pl
from jax.experimental.pallas import tpu as pltpu
from jax.sharding import PartitionSpec as P

ITERS = 4


ridge_scale = 0.05


def update(tiles, weighted, ridge, direction, along, length_sq, norm_now, solution, residual):
    scaled = weighted * along
    image = jnp.sum(tiles * scaled[None], axis=1) + ridge * direction
    curvature = jnp.sum(scaled * along, axis=0) + ridge * length_sq
    step_size = norm_now / curvature
    return (solution + step_size * direction, residual - step_size * image)


def squared_norm(values):
    partial_sum = jnp.sum(values * values, axis=0)
    return lax.psum(partial_sum, "cols")


def conjugate_plain(tiles, weighted, rating, ridge):
    target = jnp.sum(tiles * (weighted * rating)[None], axis=1)
    solution = jnp.zeros_like(target)
    residual = target
    direction = target
    norm_now = squared_norm(target)
    for iteration in range(ITERS):
        along_part = jnp.sum(tiles * direction[:, None, :], axis=0)
        length_part = jnp.sum(direction * direction, axis=0)
        along, length_sq = lax.psum((along_part, length_part), "cols")
        solution, residual = update(
            tiles, weighted, ridge, direction, along, length_sq, norm_now, solution, residual
        )
        if iteration + 1 < ITERS:
            norm_next = squared_norm(residual)
            direction = residual + norm_next / norm_now * direction
            norm_now = norm_next
    return solution


def sparse_shards(item_factors, send_list, obs_slot, obs_weight, rating, counts):
    columns = item_factors.shape[0]
    row_count = lax.axis_size("rows")
    slot_count = send_list.shape[2]
    outgoing = jnp.take(item_factors, send_list.reshape(-1), axis=1).reshape(
        columns, row_count, slot_count
    )
    arrived = lax.all_to_all(outgoing, "rows", split_axis=1, concat_axis=1, tiled=True).reshape(
        columns, row_count * slot_count
    )
    tiles = jnp.take(arrived, obs_slot, axis=1)
    present = jnp.arange(obs_slot.shape[0], dtype=jnp.int32)[:, None] < counts[None, :]
    weighted = jnp.where(present, obs_weight, jnp.float32(0.0))
    ridge = ridge_scale * counts.astype(jnp.float32)
    return conjugate_plain(tiles, weighted, rating, ridge)


def pieces_of(values, count):
    pieces = []
    for _ in range(count):
        piece = values.astype(jnp.bfloat16)
        pieces.append(piece)
        values = values - piece.astype(jnp.float32)
    return jnp.concatenate(pieces, axis=0)


def pick_kernel(col_count, factors_ref, list_ref, out_ref):
    factor_count, items = factors_ref.shape
    _, row_count, slots = list_ref.shape
    wanted = jnp.concatenate([list_ref[0, d : d + 1, :] for d in range(row_count)], axis=1)
    item = lax.broadcasted_iota(jnp.int32, (items, row_count * slots), 0)
    chosen = (item == wanted).astype(jnp.bfloat16)
    picked = jnp.dot(factors_ref[...], chosen, preferred_element_type=jnp.float32)
    group = lax.broadcasted_iota(jnp.int32, (8, 128), 1) // slots
    for d in range(row_count):
        start = d * slots
        base = start // 128 * 128
        chunk = jnp.zeros((8, 128), jnp.float32)
        for i in range(factor_count // 8):
            piece = picked[8 * i : 8 * i + 8, base : base + 128]
            shift = (slots * i - (start - base)) % 128
            if shift:
                piece = pltpu.roll(piece, shift, 1)
            chunk = jnp.where(group == i, piece, chunk)
        chunk = chunk.astype(jnp.bfloat16)
        for c in range(col_count):
            out_ref[d * col_count + c] = chunk


def spread_kernel(slot_ref, weight_ref, rating_ref, counts_ref, w_ref, b_ref, wanted):
    obs, users = slot_ref.shape
    positions = w_ref.shape[0]
    groups = obs // 8
    levels = groups.bit_length() - 1

    @pl.loop(0, users // 128)
    def _(tile):
        lanes = pl.ds(pl.multiple_of(tile * 128, 128), 128)
        row = lax.broadcasted_iota(jnp.int32, (16, 128), 0)
        live = counts_ref[:, lanes]
        for o in range(obs):
            position = jnp.where(live > o, slot_ref[o : o + 1, lanes], -1)
            wanted[16 * o : 16 * o + 16, :] = (jnp.broadcast_to(position, (16, 128)) - row).astype(jnp.int16)
        weights = [weight_ref[8 * g : 8 * g + 8, lanes] for g in range(groups)]
        ratings = [rating_ref[8 * g : 8 * g + 8, lanes] for g in range(groups)]
        named = [jnp.full((16, 128), obs, jnp.int16)] * (positions // 16)
        for o in range(obs):
            offset = wanted[16 * o : 16 * o + 16, :]
            for k in range(positions // 16):
                named[k] = jnp.where(offset == jnp.int16(16 * k), jnp.int16(o), named[k])
        for k in range(positions // 16):
            both = named[k].astype(jnp.int32)
            for half in range(2):
                slot = both[8 * half : 8 * half + 8]
                within = slot & 7
                bits = [(slot & (8 << level)) != 0 for level in range(levels)]

                def fetch(blocks):
                    found = [jnp.take_along_axis(block, within, axis=0) for block in blocks]
                    for bit in bits:
                        found = [jnp.where(bit, found[e + 1], found[e]) for e in range(0, len(found), 2)]
                    return jnp.where(slot < obs, found[0], 0.0)

                weight = fetch(weights)
                at = slice(16 * k + 8 * half, 16 * k + 8 * half + 8)
                w_ref[at, lanes] = weight
                b_ref[at, lanes] = weight * fetch(ratings)


def solve_kernel(arrived_ref, w_ref, b_ref, counts_ref, out_ref, twice_t, thrice, slots, col_count):
    own, users = out_ref.shape
    positions = w_ref.shape[0]
    factor_count = own * col_count
    row_count = positions // slots

    me = lax.axis_index("cols")
    group = lax.broadcasted_iota(jnp.int32, (8, 128), 1) // slots
    per_tile = 128 // slots
    for j in range(col_count):
        source = lax.rem(me + j, col_count)
        chunks = [arrived_ref[s * col_count + source].astype(jnp.float32) for s in range(row_count)]
        lines = []
        for i in range(own // 8):
            tiles = []
            for first in range(0, row_count, per_tile):
                tile = None
                for at in range(per_tile):
                    piece = chunks[first + at]
                    shift = (slots * (at - i)) % 128
                    if shift:
                        piece = pltpu.roll(piece, shift, 1)
                    tile = piece if tile is None else jnp.where(group == at, piece, tile)
                tiles.append(tile)
            lines.append(jnp.concatenate(tiles, axis=1))
        block = jnp.concatenate(lines, axis=0)
        for copy in range(3):
            thrice[own * j : own * (j + 1), positions * copy : positions * (copy + 1)] = block.astype(jnp.bfloat16)
    columns_t = jnp.transpose(thrice[:, :positions].astype(jnp.float32)).astype(jnp.bfloat16)
    for copy in range(2):
        twice_t[:, factor_count * copy : factor_count * (copy + 1)] = columns_t

    def dot(left, right):
        return jnp.dot(left, right, preferred_element_type=jnp.float32)

    def total(values):
        return jnp.sum(values, axis=0, keepdims=True)

    ridge = ridge_scale * counts_ref[...].astype(jnp.float32)
    residual = dot(thrice[...], pieces_of(b_ref[...], 3))
    direction = residual
    norm_now = total(residual * residual)
    result = jnp.zeros((own, users), jnp.float32)
    for iteration in range(ITERS):
        along = dot(twice_t[...], pieces_of(direction, 2))
        scaled = w_ref[...] * along
        curvature = total(scaled * along) + ridge * total(direction * direction)
        step_size = norm_now / curvature
        result = result + step_size * direction[:own]
        if iteration + 1 < ITERS:
            image = dot(thrice[...], pieces_of(scaled, 3)) + ridge * direction
            residual = residual - step_size * image
            norm_next = total(residual * residual)
            direction = residual + norm_next / norm_now * direction
            norm_now = norm_next
    out_ref[...] = result


def dense_shards(item_factors, send_list, obs_slot, obs_weight, rating, counts):
    own, items = item_factors.shape
    row_count = lax.axis_size("rows")
    col_count = lax.axis_size("cols")
    slots = send_list.shape[2]
    obs, users = obs_slot.shape
    positions = row_count * slots
    factor_count = own * col_count
    outgoing = pl.pallas_call(
        functools.partial(pick_kernel, col_count),
        out_shape=jax.ShapeDtypeStruct((row_count * col_count, 8, 128), jnp.bfloat16),
        name="pick",
    )(item_factors, send_list)
    arrived = lax.all_to_all(outgoing, ("rows", "cols"), split_axis=0, concat_axis=0, tiled=True)
    counts = counts.reshape(1, users)
    vmem = pl.BlockSpec(memory_space=pltpu.VMEM)
    by_position = pltpu.VMEM((positions, users), jnp.float32)
    weight, value = pl.pallas_call(
        spread_kernel,
        out_shape=(by_position, by_position),
        in_specs=[vmem] * 4,
        out_specs=[vmem] * 2,
        scratch_shapes=[pltpu.VMEM((16 * obs, 128), jnp.int16)],
        compiler_params=pltpu.CompilerParams(vmem_limit_bytes=16 << 20),
        cost_estimate=pl.CostEstimate(
            flops=3 * obs * positions * users, bytes_accessed=(12 * obs + 8 * positions) * users, transcendentals=0
        ),
        name="spread",
    )(obs_slot, obs_weight, rating, counts)
    return pl.pallas_call(
        functools.partial(solve_kernel, slots=slots, col_count=col_count),
        out_shape=jax.ShapeDtypeStruct((own, users), jnp.float32),
        in_specs=[vmem] * 4,
        out_specs=vmem,
        scratch_shapes=[
            pltpu.VMEM((positions, 2 * factor_count), jnp.bfloat16),
            pltpu.VMEM((factor_count, 3 * positions), jnp.bfloat16),
        ],
        compiler_params=pltpu.CompilerParams(vmem_limit_bytes=32 << 20),
        name="solve",
    )(arrived, weight, value, counts)


def shards(item_factors, send_list, obs_slot, obs_weight, rating, counts):
    positions = lax.axis_size("rows") * send_list.shape[2]
    dense = positions <= 512 and 128 % send_list.shape[2] == 0
    work = dense_shards if dense else sparse_shards
    return work(item_factors, send_list, obs_slot, obs_weight, rating, counts)


def solution(mesh):
    placed = (
        P("cols", "rows"),
        P("rows", None, None),
        P(None, "rows"),
        P(None, "rows"),
        P(None, "rows"),
        P("rows"),
    )
    return jax.shard_map(
        shards, mesh=mesh, in_specs=placed, out_specs=P("cols", "rows"), check_vma=False
    )
```

```python
import functools

import jax
import jax.numpy as jnp
from jax import lax
from jax.experimental import pallas as pl
from jax.experimental.pallas import tpu as pltpu
from jax.sharding import PartitionSpec as P

ITERS = 4


ridge_scale = 0.05


def update(tiles, weighted, ridge, direction, along, length_sq, norm_now, solution, residual):
    scaled = weighted * along
    image = jnp.sum(tiles * scaled[None], axis=1) + ridge * direction
    curvature = jnp.sum(scaled * along, axis=0) + ridge * length_sq
    step_size = norm_now / curvature
    return (solution + step_size * direction, residual - step_size * image)


def squared_norm(values):
    partial_sum = jnp.sum(values * values, axis=0)
    return lax.psum(partial_sum, "cols")


def conjugate_plain(tiles, weighted, rating, ridge):
    target = jnp.sum(tiles * (weighted * rating)[None], axis=1)
    solution = jnp.zeros_like(target)
    residual = target
    direction = target
    norm_now = squared_norm(target)
    for iteration in range(ITERS):
        along_part = jnp.sum(tiles * direction[:, None, :], axis=0)
        length_part = jnp.sum(direction * direction, axis=0)
        along, length_sq = lax.psum((along_part, length_part), "cols")
        solution, residual = update(
            tiles, weighted, ridge, direction, along, length_sq, norm_now, solution, residual
        )
        if iteration + 1 < ITERS:
            norm_next = squared_norm(residual)
            direction = residual + norm_next / norm_now * direction
            norm_now = norm_next
    return solution


def sparse_shards(item_factors, send_list, obs_slot, obs_weight, rating, counts):
    columns = item_factors.shape[0]
    row_count = lax.axis_size("rows")
    slot_count = send_list.shape[2]
    outgoing = jnp.take(item_factors, send_list.reshape(-1), axis=1).reshape(
        columns, row_count, slot_count
    )
    arrived = lax.all_to_all(outgoing, "rows", split_axis=1, concat_axis=1, tiled=True).reshape(
        columns, row_count * slot_count
    )
    tiles = jnp.take(arrived, obs_slot, axis=1)
    present = jnp.arange(obs_slot.shape[0], dtype=jnp.int32)[:, None] < counts[None, :]
    weighted = jnp.where(present, obs_weight, jnp.float32(0.0))
    ridge = ridge_scale * counts.astype(jnp.float32)
    return conjugate_plain(tiles, weighted, rating, ridge)


def pieces_of(values, count):
    pieces = []
    for _ in range(count):
        piece = values.astype(jnp.bfloat16)
        pieces.append(piece)
        values = values - piece.astype(jnp.float32)
    return jnp.concatenate(pieces, axis=0)


def pick_kernel(col_count, factors_ref, list_ref, out_ref, factors, wanted, chosen, arrived):
    factor_count, items = factors.shape
    _, row_count, slots = wanted.shape
    list_copy = pltpu.make_async_copy(list_ref, wanted, arrived.at[0])
    factors_copy = pltpu.make_async_copy(factors_ref, factors, arrived.at[1])
    list_copy.start()
    factors_copy.start()
    item = lax.broadcasted_iota(jnp.int32, (items, 128), 0).astype(jnp.int16)
    list_copy.wait()
    per_tile = 128 // slots
    for first in range(0, row_count, per_tile):
        line = jnp.concatenate([wanted[0, d : d + 1, :] for d in range(first, first + per_tile)], axis=1)
        line = jnp.broadcast_to(line, (16, 128)).astype(jnp.int16)
        line = jnp.concatenate([line] * (items // 16), axis=0)
        at = first * slots
        chosen[:, at : at + 128] = jnp.where(item == line, jnp.bfloat16(1), jnp.bfloat16(0))
    factors_copy.wait()
    picked = jnp.dot(factors[...], chosen[...], preferred_element_type=jnp.float32)
    group = lax.broadcasted_iota(jnp.int32, (8, 128), 1) // slots
    for d in range(row_count):
        start = d * slots
        base = start // 128 * 128
        chunk = jnp.zeros((8, 128), jnp.float32)
        for i in range(factor_count // 8):
            piece = picked[8 * i : 8 * i + 8, base : base + 128]
            shift = (slots * i - (start - base)) % 128
            if shift:
                piece = pltpu.roll(piece, shift, 1)
            chunk = jnp.where(group == i, piece, chunk)
        chunk = chunk.astype(jnp.bfloat16)
        for c in range(col_count):
            out_ref[d * col_count + c] = chunk


def spread_kernel(
    slot_hbm, weight_hbm, rating_hbm, counts_ref, w_ref, b_ref, ridge_ref, slot_ref, weight_ref, rating_ref, wanted, named, arrived
):
    obs, users = slot_ref.shape
    positions = w_ref.shape[0]
    groups = obs // 8
    levels = groups.bit_length() - 1
    rows = 32
    copies = [
        pltpu.make_async_copy(source, target, arrived.at[at])
        for at, (source, target) in enumerate(
            ((slot_hbm, slot_ref), (weight_hbm, weight_ref), (rating_hbm, rating_ref))
        )
    ]
    for copy in copies:
        copy.start()
    ridge_ref[...] = ridge_scale * counts_ref[...].astype(jnp.float32)
    copies[0].wait()

    @pl.loop(0, users // 128)
    def _(tile):
        lanes = pl.ds(pl.multiple_of(tile * 128, 128), 128)
        row = lax.broadcasted_iota(jnp.int32, (rows, 128), 0)
        for o in range(obs):
            position = jnp.broadcast_to(slot_ref[o : o + 1, lanes], (rows, 128))
            wanted[rows * o : rows * (o + 1), :] = (position - 128).astype(jnp.int8)
        places = [(row + (rows * k - 128)).astype(jnp.int8) for k in range(positions // rows)]
        found = [jnp.full((rows, 128), obs, jnp.int8) for _ in places]
        for o in reversed(range(obs)):
            position = wanted[rows * o : rows * (o + 1), :]
            found = [jnp.where(position == place, jnp.int8(o), last) for place, last in zip(places, found)]
        for k, slot in enumerate(found):
            named[rows * k : rows * (k + 1), lanes] = slot

    for copy in copies[1:]:
        copy.wait()

    @pl.loop(0, users // 128)
    def _(tile):
        lanes = pl.ds(pl.multiple_of(tile * 128, 128), 128)
        live = counts_ref[:, lanes]
        weights = [weight_ref[8 * g : 8 * g + 8, lanes] for g in range(groups)]
        ratings = [rating_ref[8 * g : 8 * g + 8, lanes] for g in range(groups)]
        for k in range(positions // rows):
            slots = named[rows * k : rows * (k + 1), lanes].astype(jnp.int32)
            values = []
            for at in range(0, rows, 8):
                slot = slots[at : at + 8]
                within = slot & 7
                bits = [(slot & (8 << level)) != 0 for level in range(levels)]

                def fetch(blocks):
                    picked = [jnp.take_along_axis(block, within, axis=0) for block in blocks]
                    for bit in bits:
                        picked = [jnp.where(bit, picked[e + 1], picked[e]) for e in range(0, len(picked), 2)]
                    return picked[0]

                weight = jnp.where(slot < live, fetch(weights), 0.0)
                w_ref[rows * k + at : rows * k + at + 8, lanes] = weight
                values.append(weight * fetch(ratings))
            values = jnp.concatenate(values, axis=0)
            for piece in range(2):
                part = values.astype(jnp.bfloat16)
                b_ref[positions * piece + rows * k : positions * piece + rows * (k + 1), lanes] = part
                values = values - part.astype(jnp.float32)


def solve_kernel(arrived_ref, w_ref, b_ref, ridge_ref, out_ref, twice_t, twice, slots, col_count):
    own, users = out_ref.shape
    positions = w_ref.shape[0]
    factor_count = own * col_count
    row_count = positions // slots

    me = lax.axis_index("cols")
    group = lax.broadcasted_iota(jnp.int32, (8, 128), 1) // slots
    per_tile = 128 // slots
    for j in range(col_count):
        source = lax.rem(me + j, col_count)
        chunks = [arrived_ref[s * col_count + source].astype(jnp.float32) for s in range(row_count)]
        lines = []
        for i in range(own // 8):
            tiles = []
            for first in range(0, row_count, per_tile):
                tile = None
                for at in range(per_tile):
                    piece = chunks[first + at]
                    shift = (slots * (at - i)) % 128
                    if shift:
                        piece = pltpu.roll(piece, shift, 1)
                    tile = piece if tile is None else jnp.where(group == at, piece, tile)
                tiles.append(tile)
            lines.append(jnp.concatenate(tiles, axis=1))
        block = jnp.concatenate(lines, axis=0)
        for copy in range(2):
            twice[own * j : own * (j + 1), positions * copy : positions * (copy + 1)] = block.astype(jnp.bfloat16)
    columns_t = jnp.transpose(twice[:, :positions].astype(jnp.float32)).astype(jnp.bfloat16)
    for copy in range(2):
        twice_t[:, factor_count * copy : factor_count * (copy + 1)] = columns_t

    def dot(left, right):
        return jnp.dot(left, right, preferred_element_type=jnp.float32)

    def total(values):
        return jnp.sum(values, axis=0, keepdims=True)

    ridge = ridge_ref[...]
    residual = dot(twice[...], b_ref[...])
    direction = residual
    norm_now = total(residual * residual)
    result = jnp.zeros((own, users), jnp.float32)
    for iteration in range(ITERS):
        along = dot(twice_t[...], pieces_of(direction, 2))
        scaled = w_ref[...] * along
        last = iteration + 1 == ITERS
        if last:
            curvature = total(scaled * along) + ridge * total(direction * direction)
        else:
            image = dot(twice[...], pieces_of(scaled, 2)) + ridge * direction
            curvature = total(image * direction)
        step_size = norm_now / curvature
        result = result + step_size * direction[:own]
        if not last:
            residual = residual - step_size * image
            norm_next = total(residual * residual)
            direction = residual + norm_next / norm_now * direction
            norm_now = norm_next
    out_ref[...] = result


def dense_shards(item_factors, send_list, obs_slot, obs_weight, rating, counts):
    own, items = item_factors.shape
    row_count = lax.axis_size("rows")
    col_count = lax.axis_size("cols")
    slots = send_list.shape[2]
    obs, users = obs_slot.shape
    positions = row_count * slots
    factor_count = own * col_count
    vmem = pl.BlockSpec(memory_space=pltpu.VMEM)
    hbm = pl.BlockSpec(memory_space=pltpu.HBM)

    def in_hbm(array):
        return pltpu.with_memory_space_constraint(array, pltpu.HBM)

    outgoing = pl.pallas_call(
        functools.partial(pick_kernel, col_count),
        out_shape=pltpu.VMEM((row_count * col_count, 8, 128), jnp.bfloat16),
        in_specs=[hbm] * 2,
        out_specs=vmem,
        scratch_shapes=[
            pltpu.VMEM(item_factors.shape, item_factors.dtype),
            pltpu.VMEM(send_list.shape, send_list.dtype),
            pltpu.VMEM((items, positions), jnp.bfloat16),
            pltpu.SemaphoreType.DMA((2,)),
        ],
        compiler_params=pltpu.CompilerParams(vmem_limit_bytes=4 << 20),
        name="pick",
    )(*map(in_hbm, (item_factors, send_list)))
    arrived = lax.all_to_all(outgoing, ("rows", "cols"), split_axis=0, concat_axis=0, tiled=True)
    counts = counts.reshape(1, users)
    weight, value, ridge = pl.pallas_call(
        spread_kernel,
        out_shape=(
            pltpu.VMEM((positions, users), jnp.float32),
            pltpu.VMEM((2 * positions, users), jnp.bfloat16),
            pltpu.VMEM((1, users), jnp.float32),
        ),
        in_specs=[hbm] * 3 + [vmem],
        out_specs=[vmem] * 3,
        scratch_shapes=[
            pltpu.VMEM((obs, users), jnp.int32),
            pltpu.VMEM((obs, users), jnp.float32),
            pltpu.VMEM((obs, users), jnp.float32),
            pltpu.VMEM((32 * obs, 128), jnp.int8),
            pltpu.VMEM((positions, users), jnp.int8),
            pltpu.SemaphoreType.DMA((3,)),
        ],
        compiler_params=pltpu.CompilerParams(vmem_limit_bytes=8 << 20),
        cost_estimate=pl.CostEstimate(
            flops=3 * obs * positions * users, bytes_accessed=(12 * obs + 8 * positions) * users, transcendentals=0
        ),
        name="spread",
    )(*map(in_hbm, (obs_slot, obs_weight, rating)), counts)
    return pl.pallas_call(
        functools.partial(solve_kernel, slots=slots, col_count=col_count),
        out_shape=jax.ShapeDtypeStruct((own, users), jnp.float32),
        in_specs=[vmem] * 4,
        out_specs=vmem,
        scratch_shapes=[
            pltpu.VMEM((positions, 2 * factor_count), jnp.bfloat16),
            pltpu.VMEM((factor_count, 2 * positions), jnp.bfloat16),
        ],
        compiler_params=pltpu.CompilerParams(vmem_limit_bytes=32 << 20),
        name="solve",
    )(arrived, weight, value, ridge)


def shards(item_factors, send_list, obs_slot, obs_weight, rating, counts):
    positions = lax.axis_size("rows") * send_list.shape[2]
    obs = obs_slot.shape[0]
    dense = positions <= 256 and 128 % send_list.shape[2] == 0 and obs <= 64 and obs & (obs - 1) == 0
    work = dense_shards if dense else sparse_shards
    return work(item_factors, send_list, obs_slot, obs_weight, rating, counts)


def solution(mesh):
    placed = (
        P("cols", "rows"),
        P("rows", None, None),
        P(None, "rows"),
        P(None, "rows"),
        P(None, "rows"),
        P("rows"),
    )
    return jax.shard_map(
        shards, mesh=mesh, in_specs=placed, out_specs=P("cols", "rows"), check_vma=False
    )
```

```python
import functools

import jax
import jax.numpy as jnp
from jax import lax
from jax.experimental import pallas as pl
from jax.experimental.pallas import tpu as pltpu
from jax.sharding import PartitionSpec as P

ITERS = 4


ridge_scale = 0.05


def update(tiles, weighted, ridge, direction, along, length_sq, norm_now, solution, residual):
    scaled = weighted * along
    image = jnp.sum(tiles * scaled[None], axis=1) + ridge * direction
    curvature = jnp.sum(scaled * along, axis=0) + ridge * length_sq
    step_size = norm_now / curvature
    return (solution + step_size * direction, residual - step_size * image)


def squared_norm(values):
    partial_sum = jnp.sum(values * values, axis=0)
    return lax.psum(partial_sum, "cols")


def conjugate_plain(tiles, weighted, rating, ridge):
    target = jnp.sum(tiles * (weighted * rating)[None], axis=1)
    solution = jnp.zeros_like(target)
    residual = target
    direction = target
    norm_now = squared_norm(target)
    for iteration in range(ITERS):
        along_part = jnp.sum(tiles * direction[:, None, :], axis=0)
        length_part = jnp.sum(direction * direction, axis=0)
        along, length_sq = lax.psum((along_part, length_part), "cols")
        solution, residual = update(
            tiles, weighted, ridge, direction, along, length_sq, norm_now, solution, residual
        )
        if iteration + 1 < ITERS:
            norm_next = squared_norm(residual)
            direction = residual + norm_next / norm_now * direction
            norm_now = norm_next
    return solution


def sparse_shards(item_factors, send_list, obs_slot, obs_weight, rating, counts):
    columns = item_factors.shape[0]
    row_count = lax.axis_size("rows")
    slot_count = send_list.shape[2]
    outgoing = jnp.take(item_factors, send_list.reshape(-1), axis=1).reshape(
        columns, row_count, slot_count
    )
    arrived = lax.all_to_all(outgoing, "rows", split_axis=1, concat_axis=1, tiled=True).reshape(
        columns, row_count * slot_count
    )
    tiles = jnp.take(arrived, obs_slot, axis=1)
    present = jnp.arange(obs_slot.shape[0], dtype=jnp.int32)[:, None] < counts[None, :]
    weighted = jnp.where(present, obs_weight, jnp.float32(0.0))
    ridge = ridge_scale * counts.astype(jnp.float32)
    return conjugate_plain(tiles, weighted, rating, ridge)


def pieces_of(values, count):
    pieces = []
    for _ in range(count):
        piece = values.astype(jnp.bfloat16)
        pieces.append(piece)
        values = values - piece.astype(jnp.float32)
    return jnp.concatenate(pieces, axis=0)


def swap_blocks(parts, width, wanted):
    count = 128 // width
    block = lax.broadcasted_iota(jnp.int32, (8, 128), 1) // width
    turned = []
    for shift in range(count):
        line = None
        for at in range(count):
            source = (at + shift) % count
            if source < len(parts):
                line = parts[source] if line is None else jnp.where(block == at, parts[source], line)
        turned.append(pltpu.roll(line, width * shift, 1) if shift else line)
    results = []
    for a in range(wanted):
        result = turned[-a % count]
        for b in range(1, len(parts)):
            result = jnp.where(block == b, turned[(b - a) % count], result)
        results.append(result)
    return results


def pick_kernel(col_count, factors_ref, list_ref, out_ref, factors, wanted, ready, arrived, left):
    factor_count, items = factors.shape
    _, row_count, slots = wanted.shape
    list_copy = pltpu.make_async_copy(list_ref, wanted, arrived.at[0])
    factors_copy = pltpu.make_async_copy(factors_ref, factors, arrived.at[1])
    list_copy.start()
    factors_copy.start()
    within = lax.broadcasted_iota(jnp.int32, (128, row_count * slots), 0)
    list_copy.wait()
    item = jnp.concatenate([wanted[0, d : d + 1, :] for d in range(row_count)], axis=1)
    chosen = jnp.where(within == (item & 127), jnp.float32(1), jnp.float32(0)).astype(jnp.bfloat16)
    factors_copy.wait()
    groups = items // 128
    stacked = jnp.concatenate([factors[:, 128 * g : 128 * (g + 1)] for g in range(groups)], axis=0)
    found = jnp.dot(stacked, chosen, preferred_element_type=jnp.float32)
    picked = found[:factor_count]
    for g in range(1, groups):
        picked = jnp.where(item >> 7 == g, found[factor_count * g : factor_count * (g + 1)], picked)
    per_tile = 128 // slots
    chunk_rows = 8 * col_count
    copies = []
    for first in range(0, row_count, per_tile):
        lines = picked[:, first * slots : first * slots + 128]
        parts = [lines[8 * i : 8 * i + 8] for i in range(factor_count // 8)]
        for d, chunk in enumerate(swap_blocks(parts, slots, per_tile), first):
            chunk = jnp.concatenate([chunk] * col_count, axis=0).astype(jnp.bfloat16)
            ready[chunk_rows * d : chunk_rows * (d + 1), :] = chunk
        part = pl.ds(chunk_rows * first, chunk_rows * per_tile)
        copy = pltpu.make_async_copy(ready.at[part], out_ref.at[part], left.at[len(copies)])
        copy.start()
        copies.append(copy)
    for copy in copies:
        copy.wait()


def spread_kernel(
    slot_hbm, weight_hbm, rating_hbm, counts_ref, w_ref, b_ref, slot_ref, weight_ref, rating_ref, wanted, named, arrived
):
    obs, users = slot_ref.shape
    positions = w_ref.shape[0]
    groups = obs // 8
    levels = groups.bit_length() - 1
    rows = 32
    copies = [
        pltpu.make_async_copy(source, target, arrived.at[at])
        for at, (source, target) in enumerate(
            ((slot_hbm, slot_ref), (weight_hbm, weight_ref), (rating_hbm, rating_ref))
        )
    ]
    for copy in copies:
        copy.start()
    copies[0].wait()

    @pl.loop(0, users // 128)
    def _(tile):
        lanes = pl.ds(pl.multiple_of(tile * 128, 128), 128)
        row = lax.broadcasted_iota(jnp.int32, (rows, 128), 0)
        for o in range(obs):
            position = jnp.broadcast_to(slot_ref[o : o + 1, lanes], (rows, 128))
            wanted[rows * o : rows * (o + 1), :] = (position - 128).astype(jnp.int8)
        places = [(row + (rows * k - 128)).astype(jnp.int8) for k in range(positions // rows)]
        found = [jnp.full((rows, 128), obs, jnp.int8) for _ in places]
        for o in reversed(range(obs)):
            position = wanted[rows * o : rows * (o + 1), :]
            found = [jnp.where(position == place, jnp.int8(o), last) for place, last in zip(places, found)]
        for k, slot in enumerate(found):
            named[rows * k : rows * (k + 1), lanes] = slot

    for copy in copies[1:]:
        copy.wait()

    @pl.loop(0, users // 128)
    def _(tile):
        lanes = pl.ds(pl.multiple_of(tile * 128, 128), 128)
        live = counts_ref[:, lanes]
        scale = 1.0 / (ridge_scale * live.astype(jnp.float32))
        weights = [weight_ref[8 * g : 8 * g + 8, lanes] for g in range(groups)]
        ratings = [rating_ref[8 * g : 8 * g + 8, lanes] for g in range(groups)]
        for k in range(positions // rows):
            slots = named[rows * k : rows * (k + 1), lanes].astype(jnp.int32)
            values = []
            for at in range(0, rows, 8):
                slot = slots[at : at + 8]
                within = slot & 7
                bits = [(slot & (8 << level)) != 0 for level in range(levels)]

                def fetch(blocks):
                    picked = [jnp.take_along_axis(block, within, axis=0) for block in blocks]
                    for bit in bits:
                        picked = [jnp.where(bit, picked[e + 1], picked[e]) for e in range(0, len(picked), 2)]
                    return picked[0]

                weight = jnp.where(slot < live, fetch(weights) * scale, 0.0)
                w_ref[rows * k + at : rows * k + at + 8, lanes] = weight
                values.append(weight * fetch(ratings))
            values = jnp.concatenate(values, axis=0)
            for piece in range(2):
                part = values.astype(jnp.bfloat16)
                b_ref[positions * piece + rows * k : positions * piece + rows * (k + 1), lanes] = part
                values = values - part.astype(jnp.float32)


def solve_kernel(arrived_ref, w_ref, b_ref, out_ref, unpacked, twice_t, twice, image_ref, slots, col_count):
    own, users = out_ref.shape
    positions = w_ref.shape[0]
    factor_count = own * col_count
    row_count = positions // slots

    unpacked[...] = arrived_ref[...].astype(jnp.float32)
    me = lax.axis_index("cols")
    per_tile = 128 // slots
    for j in range(col_count):
        source = lax.rem(me + j, col_count)
        chunks = [unpacked[pl.ds(8 * (s * col_count + source), 8), :] for s in range(row_count)]
        tiles = [
            jnp.concatenate(swap_blocks(chunks[first : first + per_tile], slots, own // 8), axis=0)
            for first in range(0, row_count, per_tile)
        ]
        block = jnp.concatenate(tiles, axis=1)
        for copy in range(2):
            twice[own * j : own * (j + 1), positions * copy : positions * (copy + 1)] = block.astype(jnp.bfloat16)
    columns_t = jnp.transpose(twice[:, :positions].astype(jnp.float32)).astype(jnp.bfloat16)
    for copy in range(2):
        twice_t[:, factor_count * copy : factor_count * (copy + 1)] = columns_t

    def dot(left, right):
        return jnp.dot(left, right, preferred_element_type=jnp.float32)

    def total(values):
        while values.shape[0] > 8:
            half = values.shape[0] // 2
            values = values[:half] + values[half:]
        return jnp.sum(values, axis=0, keepdims=True)

    def target(lanes):
        return dot(twice[...], b_ref[:, lanes])

    def reach(lanes, direction, last=False):
        along = dot(twice_t[...], pieces_of(direction, 2))
        scaled = w_ref[:, lanes] * along
        if last:
            return total(scaled * along)
        image_ref[:, lanes] = dot(twice[...], pieces_of(scaled, 2))
        return image_ref[:, lanes] + direction

    def advance(state, image):
        residual, direction, norm_now, length, result = state
        step_size = norm_now / total(image * direction)
        result = result + step_size * direction[:own]
        residual = residual - step_size * image
        norm_next = total(residual * residual)
        ratio = norm_next / norm_now
        return residual, residual + ratio * direction, norm_next, norm_next + ratio * ratio * length, result

    def finish(lanes, state, square):
        _, direction, norm_now, length, result = state
        out_ref[:, lanes] = result + norm_now / (square + length) * direction[:own]

    def begin(residual):
        norm_now = total(residual * residual)
        return residual, residual, norm_now, norm_now, jnp.zeros((own, residual.shape[1]), jnp.float32)

    everyone = slice(0, users)
    state = begin(target(everyone))
    for _ in range(ITERS - 1):
        state = advance(state, reach(everyone, state[1]))
    finish(everyone, state, reach(everyone, state[1], True))


def dense_shards(item_factors, send_list, obs_slot, obs_weight, rating, counts):
    own, items = item_factors.shape
    row_count = lax.axis_size("rows")
    col_count = lax.axis_size("cols")
    slots = send_list.shape[2]
    obs, users = obs_slot.shape
    positions = row_count * slots
    factor_count = own * col_count
    vmem = pl.BlockSpec(memory_space=pltpu.VMEM)
    hbm = pl.BlockSpec(memory_space=pltpu.HBM)

    def in_hbm(array):
        return pltpu.with_memory_space_constraint(array, pltpu.HBM)

    chunk_rows = 8 * row_count * col_count
    outgoing = pl.pallas_call(
        functools.partial(pick_kernel, col_count),
        out_shape=jax.ShapeDtypeStruct((chunk_rows, 128), jnp.bfloat16),
        in_specs=[hbm] * 2,
        out_specs=hbm,
        scratch_shapes=[
            pltpu.VMEM(item_factors.shape, item_factors.dtype),
            pltpu.VMEM(send_list.shape, send_list.dtype),
            pltpu.VMEM((chunk_rows, 128), jnp.bfloat16),
            pltpu.SemaphoreType.DMA((2,)),
            pltpu.SemaphoreType.DMA((positions // 128,)),
        ],
        compiler_params=pltpu.CompilerParams(vmem_limit_bytes=4 << 20),
        name="pick",
    )(*map(in_hbm, (item_factors, send_list)))
    arrived = lax.all_to_all(outgoing, ("rows", "cols"), split_axis=0, concat_axis=0, tiled=True)
    counts = counts.reshape(1, users)
    weight, value = pl.pallas_call(
        spread_kernel,
        out_shape=(
            pltpu.VMEM((positions, users), jnp.float32),
            pltpu.VMEM((2 * positions, users), jnp.bfloat16),
        ),
        in_specs=[hbm] * 3 + [vmem],
        out_specs=[vmem] * 2,
        scratch_shapes=[
            pltpu.VMEM((obs, users), jnp.int32),
            pltpu.VMEM((obs, users), jnp.float32),
            pltpu.VMEM((obs, users), jnp.float32),
            pltpu.VMEM((32 * obs, 128), jnp.int8),
            pltpu.VMEM((positions, users), jnp.int8),
            pltpu.SemaphoreType.DMA((3,)),
        ],
        compiler_params=pltpu.CompilerParams(vmem_limit_bytes=8 << 20),
        cost_estimate=pl.CostEstimate(
            flops=3 * obs * positions * users, bytes_accessed=(12 * obs + 8 * positions) * users, transcendentals=0
        ),
        name="spread",
    )(*map(in_hbm, (obs_slot, obs_weight, rating)), counts)
    return pl.pallas_call(
        functools.partial(solve_kernel, slots=slots, col_count=col_count),
        out_shape=jax.ShapeDtypeStruct((own, users), jnp.float32),
        in_specs=[vmem] * 3,
        out_specs=vmem,
        scratch_shapes=[
            pltpu.VMEM((chunk_rows, 128), jnp.float32),
            pltpu.VMEM((positions, 2 * factor_count), jnp.bfloat16),
            pltpu.VMEM((factor_count, 2 * positions), jnp.bfloat16),
            pltpu.VMEM((factor_count, users), jnp.float32),
        ],
        compiler_params=pltpu.CompilerParams(vmem_limit_bytes=32 << 20),
        name="solve",
    )(arrived, weight, value)


def shards(item_factors, send_list, obs_slot, obs_weight, rating, counts):
    positions = lax.axis_size("rows") * send_list.shape[2]
    obs = obs_slot.shape[0]
    own = item_factors.shape[0]
    packs = own % 8 == 0 and own // 8 * send_list.shape[2] <= 128
    dense = packs and positions <= 256 and positions % 128 == 0 and 128 % send_list.shape[2] == 0 and obs <= 64 and obs & (obs - 1) == 0
    work = dense_shards if dense else sparse_shards
    return work(item_factors, send_list, obs_slot, obs_weight, rating, counts)


def solution(mesh):
    placed = (
        P("cols", "rows"),
        P("rows", None, None),
        P(None, "rows"),
        P(None, "rows"),
        P(None, "rows"),
        P("rows"),
    )
    return jax.shard_map(
        shards, mesh=mesh, in_specs=placed, out_specs=P("cols", "rows"), check_vma=False
    )
```

```python
import functools
import math

import jax
import jax.numpy as jnp
from jax import lax
from jax.experimental import pallas as pl
from jax.experimental.pallas import tpu as pltpu
from jax.sharding import PartitionSpec as P

ITERS = 4


ridge_scale = 0.05


def update(tiles, weighted, ridge, direction, along, length_sq, norm_now, solution, residual):
    scaled = weighted * along
    image = jnp.sum(tiles * scaled[None], axis=1) + ridge * direction
    curvature = jnp.sum(scaled * along, axis=0) + ridge * length_sq
    step_size = norm_now / curvature
    return (solution + step_size * direction, residual - step_size * image)


def squared_norm(values):
    partial_sum = jnp.sum(values * values, axis=0)
    return lax.psum(partial_sum, "cols")


def conjugate_plain(tiles, weighted, rating, ridge):
    target = jnp.sum(tiles * (weighted * rating)[None], axis=1)
    solution = jnp.zeros_like(target)
    residual = target
    direction = target
    norm_now = squared_norm(target)
    for iteration in range(ITERS):
        along_part = jnp.sum(tiles * direction[:, None, :], axis=0)
        length_part = jnp.sum(direction * direction, axis=0)
        along, length_sq = lax.psum((along_part, length_part), "cols")
        solution, residual = update(
            tiles, weighted, ridge, direction, along, length_sq, norm_now, solution, residual
        )
        if iteration + 1 < ITERS:
            norm_next = squared_norm(residual)
            direction = residual + norm_next / norm_now * direction
            norm_now = norm_next
    return solution


def sparse_shards(item_factors, send_list, obs_slot, obs_weight, rating, counts):
    columns = item_factors.shape[0]
    row_count = lax.axis_size("rows")
    slot_count = send_list.shape[2]
    outgoing = jnp.take(item_factors, send_list.reshape(-1), axis=1).reshape(
        columns, row_count, slot_count
    )
    arrived = lax.all_to_all(outgoing, "rows", split_axis=1, concat_axis=1, tiled=True).reshape(
        columns, row_count * slot_count
    )
    tiles = jnp.take(arrived, obs_slot, axis=1)
    present = jnp.arange(obs_slot.shape[0], dtype=jnp.int32)[:, None] < counts[None, :]
    weighted = jnp.where(present, obs_weight, jnp.float32(0.0))
    ridge = ridge_scale * counts.astype(jnp.float32)
    return conjugate_plain(tiles, weighted, rating, ridge)


def pieces_of(values, count):
    pieces = []
    for _ in range(count):
        piece = values.astype(jnp.bfloat16)
        pieces.append(piece)
        values = values - piece.astype(jnp.float32)
    return jnp.concatenate(pieces, axis=0)


def swap_blocks(parts, width, wanted):
    count = 128 // width
    block = lax.broadcasted_iota(jnp.int32, (8, 128), 1) // width
    turned = []
    for shift in range(count):
        line = None
        for at in range(count):
            source = (at + shift) % count
            if source < len(parts):
                line = parts[source] if line is None else jnp.where(block == at, parts[source], line)
        turned.append(pltpu.roll(line, width * shift, 1) if shift else line)
    results = []
    for a in range(wanted):
        result = turned[-a % count]
        for b in range(1, len(parts)):
            result = jnp.where(block == b, turned[(b - a) % count], result)
        results.append(result)
    return results


def pick_kernel(col_count, factors_ref, list_ref, out_ref, factors, wanted, ready, arrived, left):
    factor_count, items = factors.shape
    _, row_count, slots = wanted.shape
    list_copy = pltpu.make_async_copy(list_ref, wanted, arrived.at[0])
    factors_copy = pltpu.make_async_copy(factors_ref, factors, arrived.at[1])
    list_copy.start()
    factors_copy.start()
    within = lax.broadcasted_iota(jnp.int32, (128, row_count * slots), 0)
    list_copy.wait()
    item = jnp.concatenate([wanted[0, d : d + 1, :] for d in range(row_count)], axis=1)
    chosen = jnp.where(within == (item & 127), jnp.float32(1), jnp.float32(0)).astype(jnp.bfloat16)
    factors_copy.wait()
    groups = items // 128
    stacked = jnp.concatenate([factors[:, 128 * g : 128 * (g + 1)] for g in range(groups)], axis=0)
    found = jnp.dot(stacked, chosen, preferred_element_type=jnp.float32)
    picked = found[:factor_count]
    for g in range(1, groups):
        picked = jnp.where(item >> 7 == g, found[factor_count * g : factor_count * (g + 1)], picked)
    per_tile = 128 // slots
    chunk_rows = 8 * col_count
    copies = []
    for first in range(0, row_count, per_tile):
        lines = picked[:, first * slots : first * slots + 128]
        parts = [lines[8 * i : 8 * i + 8] for i in range(factor_count // 8)]
        for d, chunk in enumerate(swap_blocks(parts, slots, per_tile), first):
            chunk = jnp.concatenate([chunk] * col_count, axis=0).astype(jnp.bfloat16)
            ready[chunk_rows * d : chunk_rows * (d + 1), :] = chunk
        part = pl.ds(chunk_rows * first, chunk_rows * per_tile)
        copy = pltpu.make_async_copy(ready.at[part], out_ref.at[part], left.at[len(copies)])
        copy.start()
        copies.append(copy)
    for copy in copies:
        copy.wait()


def spread_kernel(
    slot_hbm, weight_hbm, rating_hbm, counts_ref, w_ref, b_ref, slot_ref, weight_ref, rating_ref, wanted, named, arrived
):
    obs, users = slot_ref.shape
    positions = w_ref.shape[0]
    groups = obs // 8
    levels = groups.bit_length() - 1
    rows = 32
    copies = [
        pltpu.make_async_copy(source, target, arrived.at[at])
        for at, (source, target) in enumerate(
            ((slot_hbm, slot_ref), (weight_hbm, weight_ref), (rating_hbm, rating_ref))
        )
    ]
    for copy in copies:
        copy.start()
    copies[0].wait()

    @pl.loop(0, users // 128)
    def _(tile):
        lanes = pl.ds(pl.multiple_of(tile * 128, 128), 128)
        row = lax.broadcasted_iota(jnp.int32, (rows, 128), 0)
        for o in range(obs):
            position = jnp.broadcast_to(slot_ref[o : o + 1, lanes], (rows, 128))
            wanted[rows * o : rows * (o + 1), :] = (position - 128).astype(jnp.int8)
        places = [(row + (rows * k - 128)).astype(jnp.int8) for k in range(positions // rows)]
        found = [jnp.full((rows, 128), obs, jnp.int8) for _ in places]
        for o in reversed(range(obs)):
            position = wanted[rows * o : rows * (o + 1), :]
            found = [jnp.where(position == place, jnp.int8(o), last) for place, last in zip(places, found)]
        for k, slot in enumerate(found):
            named[rows * k : rows * (k + 1), lanes] = slot

    for copy in copies[1:]:
        copy.wait()

    @pl.loop(0, users // 128)
    def _(tile):
        lanes = pl.ds(pl.multiple_of(tile * 128, 128), 128)
        live = counts_ref[:, lanes]
        scale = 1.0 / (ridge_scale * live.astype(jnp.float32))
        weights = [weight_ref[8 * g : 8 * g + 8, lanes] for g in range(groups)]
        ratings = [rating_ref[8 * g : 8 * g + 8, lanes] for g in range(groups)]
        for k in range(positions // rows):
            slots = named[rows * k : rows * (k + 1), lanes].astype(jnp.int32)
            values = []
            for at in range(0, rows, 8):
                slot = slots[at : at + 8]
                within = slot & 7
                bits = [(slot & (8 << level)) != 0 for level in range(levels)]

                def fetch(blocks):
                    picked = [jnp.take_along_axis(block, within, axis=0) for block in blocks]
                    for bit in bits:
                        picked = [jnp.where(bit, picked[e + 1], picked[e]) for e in range(0, len(picked), 2)]
                    return picked[0]

                weight = jnp.where(slot < live, fetch(weights) * scale, 0.0)
                w_ref[rows * k + at : rows * k + at + 8, lanes] = weight
                values.append(weight * fetch(ratings))
            values = jnp.concatenate(values, axis=0)
            for piece in range(2):
                part = values.astype(jnp.bfloat16)
                at = rows * k // 128 * 256 + 128 * piece + rows * k % 128
                b_ref[at : at + rows, lanes] = part
                values = values - part.astype(jnp.float32)


def solve_kernel(arrived_ref, w_ref, b_ref, out_ref, unpacked, twice_t, twice, image_ref, slots, col_count):
    own, users = out_ref.shape
    positions = w_ref.shape[0]
    factor_count = own * col_count
    row_count = positions // slots

    unpacked[...] = arrived_ref[...].astype(jnp.float32)
    me = lax.axis_index("cols")
    per_tile = 128 // slots
    for j in range(col_count):
        source = lax.rem(me + j, col_count)
        chunks = [unpacked[pl.ds(8 * (s * col_count + source), 8), :] for s in range(row_count)]
        tiles = [
            jnp.concatenate(swap_blocks(chunks[first : first + per_tile], slots, own // 8), axis=0)
            for first in range(0, row_count, per_tile)
        ]
        block = jnp.concatenate(tiles, axis=1)
        for part in range(positions // 128):
            for copy in range(2):
                at = 256 * part + 128 * copy
                twice[own * j : own * (j + 1), at : at + 128] = block[:, 128 * part : 128 * part + 128].astype(jnp.bfloat16)
    for part in range(positions // 128):
        columns = twice[:, 256 * part : 256 * part + 128].astype(jnp.float32)
        columns_t = jnp.transpose(columns).astype(jnp.bfloat16)
        for copy in range(2):
            twice_t[128 * part : 128 * part + 128, factor_count * copy : factor_count * (copy + 1)] = columns_t

    def dot(left, right):
        return jnp.dot(left, right, preferred_element_type=jnp.float32)

    def total(values):
        while values.shape[0] > 8:
            half = values.shape[0] // 2
            values = values[:half] + values[half:]
        return jnp.sum(values, axis=0, keepdims=True)

    def target(lanes):
        return dot(twice[...], b_ref[:, lanes])

    def look(lanes, direction):
        along = dot(twice_t[...], pieces_of(direction, 2))
        parts = [slice(at, at + 128) for at in range(0, positions, 128)]
        return [(along[part], w_ref[part, lanes] * along[part]) for part in parts]

    def square(views):
        return sum(total(scaled * along) for along, scaled in views)

    def back(lanes, views, direction):
        pieces = jnp.concatenate([pieces_of(scaled, 2) for _, scaled in views], axis=0)
        image_ref[:, lanes] = dot(twice[...], pieces)
        return image_ref[:, lanes] + direction

    def advance(state, image):
        residual, direction, norm_now, length, result = state
        step_size = norm_now / total(image * direction)
        result = result + step_size * direction[:own]
        residual = residual - step_size * image
        norm_next = total(residual * residual)
        ratio = norm_next / norm_now
        return residual, residual + ratio * direction, norm_next, norm_next + ratio * ratio * length, result

    def finish(lanes, state, square):
        _, direction, norm_now, length, result = state
        out_ref[:, lanes] = result + norm_now / (square + length) * direction[:own]

    def begin(residual):
        norm_now = total(residual * residual)
        return residual, residual, norm_now, norm_now, jnp.zeros((own, residual.shape[1]), jnp.float32)

    width = math.gcd(users, 256)
    groups = [slice(at, at + width) for at in range(0, users, width)]
    states = [begin(target(lanes)) for lanes in groups]
    for _ in range(ITERS - 1):
        images = [back(lanes, look(lanes, state[1]), state[1]) for lanes, state in zip(groups, states)]
        states = [advance(state, image) for state, image in zip(states, images)]
    for lanes, state in zip(groups, states):
        finish(lanes, state, square(look(lanes, state[1])))


def dense_shards(item_factors, send_list, obs_slot, obs_weight, rating, counts):
    own, items = item_factors.shape
    row_count = lax.axis_size("rows")
    col_count = lax.axis_size("cols")
    slots = send_list.shape[2]
    obs, users = obs_slot.shape
    positions = row_count * slots
    factor_count = own * col_count
    vmem = pl.BlockSpec(memory_space=pltpu.VMEM)
    hbm = pl.BlockSpec(memory_space=pltpu.HBM)

    def in_hbm(array):
        return pltpu.with_memory_space_constraint(array, pltpu.HBM)

    chunk_rows = 8 * row_count * col_count
    outgoing = pl.pallas_call(
        functools.partial(pick_kernel, col_count),
        out_shape=jax.ShapeDtypeStruct((chunk_rows, 128), jnp.bfloat16),
        in_specs=[hbm] * 2,
        out_specs=hbm,
        scratch_shapes=[
            pltpu.VMEM(item_factors.shape, item_factors.dtype),
            pltpu.VMEM(send_list.shape, send_list.dtype),
            pltpu.VMEM((chunk_rows, 128), jnp.bfloat16),
            pltpu.SemaphoreType.DMA((2,)),
            pltpu.SemaphoreType.DMA((positions // 128,)),
        ],
        compiler_params=pltpu.CompilerParams(vmem_limit_bytes=4 << 20),
        name="pick",
    )(*map(in_hbm, (item_factors, send_list)))
    arrived = lax.all_to_all(outgoing, ("rows", "cols"), split_axis=0, concat_axis=0, tiled=True)
    counts = counts.reshape(1, users)
    weight, value = pl.pallas_call(
        spread_kernel,
        out_shape=(
            pltpu.VMEM((positions, users), jnp.float32),
            pltpu.VMEM((2 * positions, users), jnp.bfloat16),
        ),
        in_specs=[hbm] * 3 + [vmem],
        out_specs=[vmem] * 2,
        scratch_shapes=[
            pltpu.VMEM((obs, users), jnp.int32),
            pltpu.VMEM((obs, users), jnp.float32),
            pltpu.VMEM((obs, users), jnp.float32),
            pltpu.VMEM((32 * obs, 128), jnp.int8),
            pltpu.VMEM((positions, users), jnp.int8),
            pltpu.SemaphoreType.DMA((3,)),
        ],
        compiler_params=pltpu.CompilerParams(vmem_limit_bytes=8 << 20),
        cost_estimate=pl.CostEstimate(
            flops=3 * obs * positions * users, bytes_accessed=(12 * obs + 8 * positions) * users, transcendentals=0
        ),
        name="spread",
    )(*map(in_hbm, (obs_slot, obs_weight, rating)), counts)
    return pl.pallas_call(
        functools.partial(solve_kernel, slots=slots, col_count=col_count),
        out_shape=jax.ShapeDtypeStruct((own, users), jnp.float32),
        in_specs=[vmem] * 3,
        out_specs=vmem,
        scratch_shapes=[
            pltpu.VMEM((chunk_rows, 128), jnp.float32),
            pltpu.VMEM((positions, 2 * factor_count), jnp.bfloat16),
            pltpu.VMEM((factor_count, 2 * positions), jnp.bfloat16),
            pltpu.VMEM((factor_count, users), jnp.float32),
        ],
        compiler_params=pltpu.CompilerParams(vmem_limit_bytes=32 << 20),
        name="solve",
    )(arrived, weight, value)


def shards(item_factors, send_list, obs_slot, obs_weight, rating, counts):
    positions = lax.axis_size("rows") * send_list.shape[2]
    obs = obs_slot.shape[0]
    own = item_factors.shape[0]
    packs = own % 8 == 0 and own // 8 * send_list.shape[2] <= 128
    dense = packs and positions <= 256 and positions % 128 == 0 and 128 % send_list.shape[2] == 0 and obs <= 64 and obs & (obs - 1) == 0
    work = dense_shards if dense else sparse_shards
    return work(item_factors, send_list, obs_slot, obs_weight, rating, counts)


def solution(mesh):
    placed = (
        P("cols", "rows"),
        P("rows", None, None),
        P(None, "rows"),
        P(None, "rows"),
        P(None, "rows"),
        P("rows"),
    )
    return jax.shard_map(
        shards, mesh=mesh, in_specs=placed, out_specs=P("cols", "rows"), check_vma=False
    )
```

```python
import functools
import math

import jax
import jax.numpy as jnp
from jax import lax
from jax.experimental import pallas as pl
from jax.experimental.pallas import tpu as pltpu
from jax.sharding import PartitionSpec as P

ITERS = 4


ridge_scale = 0.05


def update(tiles, weighted, ridge, direction, along, length_sq, norm_now, solution, residual):
    scaled = weighted * along
    image = jnp.sum(tiles * scaled[None], axis=1) + ridge * direction
    curvature = jnp.sum(scaled * along, axis=0) + ridge * length_sq
    step_size = norm_now / curvature
    return (solution + step_size * direction, residual - step_size * image)


def squared_norm(values):
    partial_sum = jnp.sum(values * values, axis=0)
    return lax.psum(partial_sum, "cols")


def conjugate_plain(tiles, weighted, rating, ridge):
    target = jnp.sum(tiles * (weighted * rating)[None], axis=1)
    solution = jnp.zeros_like(target)
    residual = target
    direction = target
    norm_now = squared_norm(target)
    for iteration in range(ITERS):
        along_part = jnp.sum(tiles * direction[:, None, :], axis=0)
        length_part = jnp.sum(direction * direction, axis=0)
        along, length_sq = lax.psum((along_part, length_part), "cols")
        solution, residual = update(
            tiles, weighted, ridge, direction, along, length_sq, norm_now, solution, residual
        )
        if iteration + 1 < ITERS:
            norm_next = squared_norm(residual)
            direction = residual + norm_next / norm_now * direction
            norm_now = norm_next
    return solution


def sparse_shards(item_factors, send_list, obs_slot, obs_weight, rating, counts):
    columns = item_factors.shape[0]
    row_count = lax.axis_size("rows")
    slot_count = send_list.shape[2]
    outgoing = jnp.take(item_factors, send_list.reshape(-1), axis=1).reshape(
        columns, row_count, slot_count
    )
    arrived = lax.all_to_all(outgoing, "rows", split_axis=1, concat_axis=1, tiled=True).reshape(
        columns, row_count * slot_count
    )
    tiles = jnp.take(arrived, obs_slot, axis=1)
    present = jnp.arange(obs_slot.shape[0], dtype=jnp.int32)[:, None] < counts[None, :]
    weighted = jnp.where(present, obs_weight, jnp.float32(0.0))
    ridge = ridge_scale * counts.astype(jnp.float32)
    return conjugate_plain(tiles, weighted, rating, ridge)


def pieces_of(values, count):
    pieces = []
    for _ in range(count):
        piece = values.astype(jnp.bfloat16)
        pieces.append(piece)
        values = values - piece.astype(jnp.float32)
    return jnp.concatenate(pieces, axis=0)


def swap_blocks(parts, width, wanted):
    count = 128 // width
    block = lax.broadcasted_iota(jnp.int32, (8, 128), 1) // width
    turned = []
    for shift in range(count):
        line = None
        for at in range(count):
            source = (at + shift) % count
            if source < len(parts):
                line = parts[source] if line is None else jnp.where(block == at, parts[source], line)
        turned.append(pltpu.roll(line, width * shift, 1) if shift else line)
    results = []
    for a in range(wanted):
        result = turned[-a % count]
        for b in range(1, len(parts)):
            result = jnp.where(block == b, turned[(b - a) % count], result)
        results.append(result)
    return results


def pick_kernel(col_count, factors_ref, list_ref, out_ref, factors, wanted, ready, arrived, left):
    factor_count, items = factors.shape
    _, row_count, slots = wanted.shape
    list_copy = pltpu.make_async_copy(list_ref, wanted, arrived.at[0])
    quarter = items // 4
    factors_copies = []
    for part in range(4):
        lanes = pl.ds(quarter * part, quarter)
        factors_copies.append(
            pltpu.make_async_copy(factors_ref.at[:, lanes], factors.at[:, lanes], arrived.at[1 + part])
        )
    list_copy.start()
    for copy in factors_copies:
        copy.start()
    within = lax.broadcasted_iota(jnp.int32, (128, row_count * slots), 0)
    list_copy.wait()
    item = jnp.concatenate([wanted[0, d : d + 1, :] for d in range(row_count)], axis=1)
    chosen = jnp.where(within == (item & 127), jnp.float32(1), jnp.float32(0)).astype(jnp.bfloat16)
    for copy in factors_copies:
        copy.wait()
    groups = items // 128
    stacked = jnp.concatenate([factors[:, 128 * g : 128 * (g + 1)] for g in range(groups)], axis=0)
    found = jnp.dot(stacked, chosen, preferred_element_type=jnp.float32)
    picked = found[:factor_count]
    for g in range(1, groups):
        picked = jnp.where(item >> 7 == g, found[factor_count * g : factor_count * (g + 1)], picked)
    per_tile = 128 // slots
    chunk_rows = 8 * col_count
    copies = []
    for first in range(0, row_count, per_tile):
        lines = picked[:, first * slots : first * slots + 128]
        parts = [lines[8 * i : 8 * i + 8] for i in range(factor_count // 8)]
        for d, chunk in enumerate(swap_blocks(parts, slots, per_tile), first):
            chunk = jnp.concatenate([chunk] * col_count, axis=0).astype(jnp.bfloat16)
            ready[chunk_rows * d : chunk_rows * (d + 1), :] = chunk
        half = chunk_rows * per_tile // 2
        for start in (chunk_rows * first, chunk_rows * first + half):
            part = pl.ds(start, half)
            copy = pltpu.make_async_copy(ready.at[part], out_ref.at[part], left.at[len(copies)])
            copy.start()
            copies.append(copy)
    for copy in copies:
        copy.wait()


def spread_kernel(
    slot_hbm, weight_hbm, rating_hbm, counts_hbm, w_ref, b_ref,
    slot_ref, weight_ref, rating_ref, counts_ref, wanted, named, arrived
):
    obs, users = slot_ref.shape
    positions = w_ref.shape[0]
    groups = obs // 8
    levels = groups.bit_length() - 1
    rows = 32
    copies = [
        pltpu.make_async_copy(source, target, arrived.at[at])
        for at, (source, target) in enumerate(
            ((slot_hbm, slot_ref), (weight_hbm, weight_ref), (rating_hbm, rating_ref), (counts_hbm, counts_ref))
        )
    ]
    for copy in copies:
        copy.start()
    copies[0].wait()

    @pl.loop(0, users // 128)
    def _(tile):
        lanes = pl.ds(pl.multiple_of(tile * 128, 128), 128)
        row = lax.broadcasted_iota(jnp.int32, (rows, 128), 0)
        for o in range(obs):
            position = jnp.broadcast_to(slot_ref[o : o + 1, lanes], (rows, 128))
            wanted[rows * o : rows * (o + 1), :] = (position - 128).astype(jnp.int8)
        places = [(row + (rows * k - 128)).astype(jnp.int8) for k in range(positions // rows)]
        found = [jnp.full((rows, 128), obs, jnp.int8) for _ in places]
        for o in reversed(range(obs)):
            position = wanted[rows * o : rows * (o + 1), :]
            found = [jnp.where(position == place, jnp.int8(o), last) for place, last in zip(places, found)]
        for k, slot in enumerate(found):
            named[rows * k : rows * (k + 1), lanes] = slot

    for copy in copies[1:]:
        copy.wait()

    @pl.loop(0, users // 128)
    def _(tile):
        lanes = pl.ds(pl.multiple_of(tile * 128, 128), 128)
        live = counts_ref[:, lanes]
        scale = 1.0 / (ridge_scale * live.astype(jnp.float32))
        weights = [weight_ref[8 * g : 8 * g + 8, lanes] for g in range(groups)]
        ratings = [rating_ref[8 * g : 8 * g + 8, lanes] for g in range(groups)]
        for k in range(positions // rows):
            slots = named[rows * k : rows * (k + 1), lanes].astype(jnp.int32)
            values = []
            for at in range(0, rows, 8):
                slot = slots[at : at + 8]
                within = slot & 7
                bits = [(slot & (8 << level)) != 0 for level in range(levels)]

                def fetch(blocks):
                    picked = [jnp.take_along_axis(block, within, axis=0) for block in blocks]
                    for bit in bits:
                        picked = [jnp.where(bit, picked[e + 1], picked[e]) for e in range(0, len(picked), 2)]
                    return picked[0]

                weight = jnp.where(slot < live, fetch(weights) * scale, 0.0)
                w_ref[rows * k + at : rows * k + at + 8, lanes] = weight
                values.append(weight * fetch(ratings))
            values = jnp.concatenate(values, axis=0)
            for piece in range(2):
                part = values.astype(jnp.bfloat16)
                at = rows * k // 128 * 256 + 128 * piece + rows * k % 128
                b_ref[at : at + rows, lanes] = part
                values = values - part.astype(jnp.float32)


def solve_kernel(arrived_ref, w_ref, b_ref, out_ref, unpacked, twice_t, twice, image_ref, slots, col_count):
    own, users = out_ref.shape
    positions = w_ref.shape[0]
    factor_count = own * col_count
    row_count = positions // slots

    unpacked[...] = arrived_ref[...].astype(jnp.float32)
    me = lax.axis_index("cols")
    per_tile = 128 // slots
    for j in range(col_count):
        source = lax.rem(me + j, col_count)
        chunks = [unpacked[pl.ds(8 * (s * col_count + source), 8), :] for s in range(row_count)]
        tiles = [
            jnp.concatenate(swap_blocks(chunks[first : first + per_tile], slots, own // 8), axis=0)
            for first in range(0, row_count, per_tile)
        ]
        block = jnp.concatenate(tiles, axis=1)
        for part in range(positions // 128):
            for copy in range(2):
                at = 256 * part + 128 * copy
                twice[own * j : own * (j + 1), at : at + 128] = block[:, 128 * part : 128 * part + 128].astype(jnp.bfloat16)
    for part in range(positions // 128):
        columns = twice[:, 256 * part : 256 * part + 128].astype(jnp.float32)
        columns_t = jnp.transpose(columns).astype(jnp.bfloat16)
        for copy in range(2):
            twice_t[128 * part : 128 * part + 128, factor_count * copy : factor_count * (copy + 1)] = columns_t

    def dot(left, right):
        return jnp.dot(left, right, preferred_element_type=jnp.float32)

    def total(values):
        while values.shape[0] > 8:
            half = values.shape[0] // 2
            values = values[:half] + values[half:]
        return jnp.sum(values, axis=0, keepdims=True)

    def target(lanes):
        return dot(twice[...], b_ref[:, lanes])

    def look(lanes, direction):
        along = dot(twice_t[...], pieces_of(direction, 2))
        parts = [slice(at, at + 128) for at in range(0, positions, 128)]
        return [(along[part], w_ref[part, lanes] * along[part]) for part in parts]

    def square(views):
        return sum(total(scaled * along) for along, scaled in views)

    def back(lanes, views, direction):
        pieces = jnp.concatenate([pieces_of(scaled, 2) for _, scaled in views], axis=0)
        image_ref[:, lanes] = dot(twice[...], pieces)
        return image_ref[:, lanes] + direction

    def advance(state, image):
        residual, direction, norm_now, length, result = state
        step_size = norm_now / total(image * direction)
        result = result + step_size * direction[:own]
        residual = residual - step_size * image
        norm_next = total(residual * residual)
        ratio = norm_next / norm_now
        return residual, residual + ratio * direction, norm_next, norm_next + ratio * ratio * length, result

    def finish(lanes, state, square):
        _, direction, norm_now, length, result = state
        out_ref[:, lanes] = result + norm_now / (square + length) * direction[:own]

    def begin(residual):
        norm_now = total(residual * residual)
        return residual, residual, norm_now, norm_now, jnp.zeros((own, residual.shape[1]), jnp.float32)

    width = math.gcd(users, 256)
    groups = [slice(at, at + width) for at in range(0, users, width)]
    states = [begin(target(lanes)) for lanes in groups]
    for _ in range(ITERS - 1):
        images = [back(lanes, look(lanes, state[1]), state[1]) for lanes, state in zip(groups, states)]
        states = [advance(state, image) for state, image in zip(states, images)]
    for lanes, state in zip(groups, states):
        finish(lanes, state, square(look(lanes, state[1])))


def dense_shards(item_factors, send_list, obs_slot, obs_weight, rating, counts):
    own, items = item_factors.shape
    row_count = lax.axis_size("rows")
    col_count = lax.axis_size("cols")
    slots = send_list.shape[2]
    obs, users = obs_slot.shape
    positions = row_count * slots
    factor_count = own * col_count
    vmem = pl.BlockSpec(memory_space=pltpu.VMEM)
    hbm = pl.BlockSpec(memory_space=pltpu.HBM)

    def in_hbm(array):
        return pltpu.with_memory_space_constraint(array, pltpu.HBM)

    chunk_rows = 8 * row_count * col_count
    outgoing = pl.pallas_call(
        functools.partial(pick_kernel, col_count),
        out_shape=jax.ShapeDtypeStruct((chunk_rows, 128), jnp.bfloat16),
        in_specs=[hbm] * 2,
        out_specs=hbm,
        scratch_shapes=[
            pltpu.VMEM(item_factors.shape, item_factors.dtype),
            pltpu.VMEM(send_list.shape, send_list.dtype),
            pltpu.VMEM((chunk_rows, 128), jnp.bfloat16),
            pltpu.SemaphoreType.DMA((5,)),
            pltpu.SemaphoreType.DMA((2 * positions // 128,)),
        ],
        compiler_params=pltpu.CompilerParams(vmem_limit_bytes=4 << 20),
        name="pick",
    )(*map(in_hbm, (item_factors, send_list)))
    arrived = lax.all_to_all(outgoing, ("rows", "cols"), split_axis=0, concat_axis=0, tiled=True)
    counts = counts.reshape(1, users)
    weight, value = pl.pallas_call(
        spread_kernel,
        out_shape=(
            pltpu.VMEM((positions, users), jnp.float32),
            pltpu.VMEM((2 * positions, users), jnp.bfloat16),
        ),
        in_specs=[hbm] * 4,
        out_specs=[vmem] * 2,
        scratch_shapes=[
            pltpu.VMEM((obs, users), jnp.int32),
            pltpu.VMEM((obs, users), jnp.float32),
            pltpu.VMEM((obs, users), jnp.float32),
            pltpu.VMEM((1, users), jnp.int32),
            pltpu.VMEM((32 * obs, 128), jnp.int8),
            pltpu.VMEM((positions, users), jnp.int8),
            pltpu.SemaphoreType.DMA((4,)),
        ],
        compiler_params=pltpu.CompilerParams(vmem_limit_bytes=8 << 20),
        cost_estimate=pl.CostEstimate(
            flops=3 * obs * positions * users, bytes_accessed=(12 * obs + 8 * positions) * users, transcendentals=0
        ),
        name="spread",
    )(*map(in_hbm, (obs_slot, obs_weight, rating, counts)))
    return pl.pallas_call(
        functools.partial(solve_kernel, slots=slots, col_count=col_count),
        out_shape=jax.ShapeDtypeStruct((own, users), jnp.float32),
        in_specs=[vmem] * 3,
        out_specs=vmem,
        scratch_shapes=[
            pltpu.VMEM((chunk_rows, 128), jnp.float32),
            pltpu.VMEM((positions, 2 * factor_count), jnp.bfloat16),
            pltpu.VMEM((factor_count, 2 * positions), jnp.bfloat16),
            pltpu.VMEM((factor_count, users), jnp.float32),
        ],
        compiler_params=pltpu.CompilerParams(vmem_limit_bytes=32 << 20),
        name="solve",
    )(arrived, weight, value)


def shards(item_factors, send_list, obs_slot, obs_weight, rating, counts):
    positions = lax.axis_size("rows") * send_list.shape[2]
    obs = obs_slot.shape[0]
    own = item_factors.shape[0]
    packs = own % 8 == 0 and own // 8 * send_list.shape[2] <= 128
    dense = packs and positions <= 256 and positions % 128 == 0 and 128 % send_list.shape[2] == 0 and obs <= 64 and obs & (obs - 1) == 0
    work = dense_shards if dense else sparse_shards
    return work(item_factors, send_list, obs_slot, obs_weight, rating, counts)


def solution(mesh):
    placed = (
        P("cols", "rows"),
        P("rows", None, None),
        P(None, "rows"),
        P(None, "rows"),
        P(None, "rows"),
        P("rows"),
    )
    return jax.shard_map(
        shards, mesh=mesh, in_specs=placed, out_specs=P("cols", "rows"), check_vma=False
    )
```

```python
import functools
import math

import jax
import jax.numpy as jnp
from jax import lax
from jax.experimental import pallas as pl
from jax.experimental.pallas import tpu as pltpu
from jax.sharding import PartitionSpec as P

ITERS = 4


ridge_scale = 0.05


def update(tiles, weighted, ridge, direction, along, length_sq, norm_now, solution, residual):
    scaled = weighted * along
    image = jnp.sum(tiles * scaled[None], axis=1) + ridge * direction
    curvature = jnp.sum(scaled * along, axis=0) + ridge * length_sq
    step_size = norm_now / curvature
    return (solution + step_size * direction, residual - step_size * image)


def squared_norm(values):
    partial_sum = jnp.sum(values * values, axis=0)
    return lax.psum(partial_sum, "cols")


def conjugate_plain(tiles, weighted, rating, ridge):
    target = jnp.sum(tiles * (weighted * rating)[None], axis=1)
    solution = jnp.zeros_like(target)
    residual = target
    direction = target
    norm_now = squared_norm(target)
    for iteration in range(ITERS):
        along_part = jnp.sum(tiles * direction[:, None, :], axis=0)
        length_part = jnp.sum(direction * direction, axis=0)
        along, length_sq = lax.psum((along_part, length_part), "cols")
        solution, residual = update(
            tiles, weighted, ridge, direction, along, length_sq, norm_now, solution, residual
        )
        if iteration + 1 < ITERS:
            norm_next = squared_norm(residual)
            direction = residual + norm_next / norm_now * direction
            norm_now = norm_next
    return solution


def sparse_shards(item_factors, send_list, obs_slot, obs_weight, rating, counts):
    columns = item_factors.shape[0]
    row_count = lax.axis_size("rows")
    slot_count = send_list.shape[2]
    outgoing = jnp.take(item_factors, send_list.reshape(-1), axis=1).reshape(
        columns, row_count, slot_count
    )
    arrived = lax.all_to_all(outgoing, "rows", split_axis=1, concat_axis=1, tiled=True).reshape(
        columns, row_count * slot_count
    )
    tiles = jnp.take(arrived, obs_slot, axis=1)
    present = jnp.arange(obs_slot.shape[0], dtype=jnp.int32)[:, None] < counts[None, :]
    weighted = jnp.where(present, obs_weight, jnp.float32(0.0))
    ridge = ridge_scale * counts.astype(jnp.float32)
    return conjugate_plain(tiles, weighted, rating, ridge)


def pieces_of(values, count):
    pieces = []
    for _ in range(count):
        piece = values.astype(jnp.bfloat16)
        pieces.append(piece)
        values = values - piece.astype(jnp.float32)
    return jnp.concatenate(pieces, axis=0)


def swap_blocks(parts, width, wanted):
    count = 128 // width
    block = lax.broadcasted_iota(jnp.int32, (8, 128), 1) // width
    turned = []
    for shift in range(count):
        line = None
        for at in range(count):
            source = (at + shift) % count
            if source < len(parts):
                line = parts[source] if line is None else jnp.where(block == at, parts[source], line)
        turned.append(pltpu.roll(line, width * shift, 1) if shift else line)
    results = []
    for a in range(wanted):
        result = turned[-a % count]
        for b in range(1, len(parts)):
            result = jnp.where(block == b, turned[(b - a) % count], result)
        results.append(result)
    return results


def pick_kernel(col_count, factors_ref, list_ref, out_ref, factors, wanted, ready, arrived, left):
    factor_count, items = factors.shape
    _, row_count, slots = wanted.shape
    list_copy = pltpu.make_async_copy(list_ref, wanted, arrived.at[0])
    quarter = items // 4
    factors_copies = []
    for part in range(4):
        lanes = pl.ds(quarter * part, quarter)
        factors_copies.append(
            pltpu.make_async_copy(factors_ref.at[:, lanes], factors.at[:, lanes], arrived.at[1 + part])
        )
    list_copy.start()
    for copy in factors_copies:
        copy.start()
    within = lax.broadcasted_iota(jnp.int32, (128, row_count * slots), 0)
    list_copy.wait()
    item = jnp.concatenate([wanted[0, d : d + 1, :] for d in range(row_count)], axis=1)
    chosen = jnp.where(within == (item & 127), jnp.float32(1), jnp.float32(0)).astype(jnp.bfloat16)
    for copy in factors_copies:
        copy.wait()
    groups = items // 128
    stacked = jnp.concatenate([factors[:, 128 * g : 128 * (g + 1)] for g in range(groups)], axis=0)
    found = jnp.dot(stacked, chosen, preferred_element_type=jnp.float32)
    picked = found[:factor_count]
    for g in range(1, groups):
        picked = jnp.where(item >> 7 == g, found[factor_count * g : factor_count * (g + 1)], picked)
    per_tile = 128 // slots
    chunk_rows = 8 * col_count
    copies = []
    for first in range(0, row_count, per_tile):
        lines = picked[:, first * slots : first * slots + 128]
        parts = [lines[8 * i : 8 * i + 8] for i in range(factor_count // 8)]
        for d, chunk in enumerate(swap_blocks(parts, slots, per_tile), first):
            chunk = jnp.concatenate([chunk] * col_count, axis=0).astype(jnp.bfloat16)
            ready[chunk_rows * d : chunk_rows * (d + 1), :] = chunk
        half = chunk_rows * per_tile // 2
        for start in (chunk_rows * first, chunk_rows * first + half):
            part = pl.ds(start, half)
            copy = pltpu.make_async_copy(ready.at[part], out_ref.at[part], left.at[len(copies)])
            copy.start()
            copies.append(copy)
    for copy in copies:
        copy.wait()


def spread_kernel(
    slot_hbm, weight_hbm, rating_hbm, counts_hbm, w_ref, b_ref,
    slot_ref, weight_ref, rating_ref, counts_ref, wanted, named, arrived
):
    obs, users = slot_ref.shape
    positions = w_ref.shape[0]
    groups = obs // 8
    levels = groups.bit_length() - 1
    rows = 32
    copies = [
        pltpu.make_async_copy(source, target, arrived.at[at])
        for at, (source, target) in enumerate(
            ((slot_hbm, slot_ref), (weight_hbm, weight_ref), (rating_hbm, rating_ref), (counts_hbm, counts_ref))
        )
    ]
    for copy in copies:
        copy.start()
    copies[0].wait()

    @pl.loop(0, users // 128)
    def _(tile):
        lanes = pl.ds(pl.multiple_of(tile * 128, 128), 128)
        row = lax.broadcasted_iota(jnp.int32, (rows, 128), 0)
        for o in range(obs):
            position = jnp.broadcast_to(slot_ref[o : o + 1, lanes], (rows, 128))
            wanted[rows * o : rows * (o + 1), :] = (position - 128).astype(jnp.int8)
        places = [(row + (rows * k - 128)).astype(jnp.int8) for k in range(positions // rows)]
        found = [jnp.full((rows, 128), obs, jnp.int8) for _ in places]
        for o in reversed(range(obs)):
            position = wanted[rows * o : rows * (o + 1), :]
            found = [jnp.where(position == place, jnp.int8(o), last) for place, last in zip(places, found)]
        for k, slot in enumerate(found):
            named[rows * k : rows * (k + 1), lanes] = slot

    for copy in copies[1:]:
        copy.wait()

    @pl.loop(0, users // 128)
    def _(tile):
        lanes = pl.ds(pl.multiple_of(tile * 128, 128), 128)
        live = counts_ref[:, lanes]
        scale = 1.0 / (ridge_scale * live.astype(jnp.float32))
        weights = [weight_ref[8 * g : 8 * g + 8, lanes] for g in range(groups)]
        ratings = [rating_ref[8 * g : 8 * g + 8, lanes] for g in range(groups)]
        for k in range(positions // rows):
            slots = named[rows * k : rows * (k + 1), lanes].astype(jnp.int32)
            values = []
            for at in range(0, rows, 8):
                slot = slots[at : at + 8]
                within = slot & 7
                bits = [(slot & (8 << level)) != 0 for level in range(levels)]

                def fetch(blocks):
                    picked = [jnp.take_along_axis(block, within, axis=0) for block in blocks]
                    for bit in bits:
                        picked = [jnp.where(bit, picked[e + 1], picked[e]) for e in range(0, len(picked), 2)]
                    return picked[0]

                weight = jnp.where(slot < live, fetch(weights) * scale, 0.0)
                w_ref[rows * k + at : rows * k + at + 8, lanes] = weight
                values.append(weight * fetch(ratings))
            values = jnp.concatenate(values, axis=0)
            for piece in range(2):
                part = values.astype(jnp.bfloat16)
                at = rows * k // 128 * 256 + 128 * piece + rows * k % 128
                b_ref[at : at + rows, lanes] = part
                values = values - part.astype(jnp.float32)


def solve_kernel(arrived_ref, w_ref, b_ref, out_ref, unpacked, twice_t, twice, image_ref, slots, col_count):
    own, users = out_ref.shape
    positions = w_ref.shape[0]
    factor_count = own * col_count
    row_count = positions // slots

    unpacked[...] = arrived_ref[...].astype(jnp.float32)
    me = lax.axis_index("cols")
    per_tile = 128 // slots
    for j in range(col_count):
        source = lax.rem(me + j, col_count)
        chunks = [unpacked[pl.ds(8 * (s * col_count + source), 8), :] for s in range(row_count)]
        tiles = [
            jnp.concatenate(swap_blocks(chunks[first : first + per_tile], slots, own // 8), axis=0)
            for first in range(0, row_count, per_tile)
        ]
        block = jnp.concatenate(tiles, axis=1)
        for part in range(positions // 128):
            for copy in range(2):
                at = 256 * part + 128 * copy
                twice[own * j : own * (j + 1), at : at + 128] = block[:, 128 * part : 128 * part + 128].astype(jnp.bfloat16)
    for part in range(positions // 128):
        columns = twice[:, 256 * part : 256 * part + 128].astype(jnp.float32)
        columns_t = jnp.transpose(columns).astype(jnp.bfloat16)
        for copy in range(2):
            twice_t[128 * part : 128 * part + 128, factor_count * copy : factor_count * (copy + 1)] = columns_t

    def dot(left, right):
        return jnp.dot(left, right, preferred_element_type=jnp.float32)

    def total(values):
        while values.shape[0] > 8:
            half = values.shape[0] // 2
            values = values[:half] + values[half:]
        return jnp.sum(values, axis=0, keepdims=True)

    def target(lanes):
        return dot(twice[...], b_ref[:, lanes])

    def look(lanes, direction):
        along = dot(twice_t[...], pieces_of(direction, 2))
        parts = [slice(at, at + 128) for at in range(0, positions, 128)]
        return [(along[part], w_ref[part, lanes] * along[part]) for part in parts]

    def square(lanes, direction):
        pieces = pieces_of(direction, 2)
        parts = [slice(at, at + 128) for at in range(0, positions, 128)]
        views = [(dot(twice_t[part], pieces), w_ref[part, lanes]) for part in parts]
        return sum(total(weight * along * along) for along, weight in views)

    def back(lanes, views, direction):
        pieces = jnp.concatenate([pieces_of(scaled, 2) for _, scaled in views], axis=0)
        image_ref[:, lanes] = dot(twice[...], pieces)
        return image_ref[:, lanes] + direction

    def advance(state, image):
        residual, direction, norm_now, length, result = state
        step_size = norm_now / total(image * direction)
        result = result + step_size * direction[:own]
        residual = residual - step_size * image
        norm_next = total(residual * residual)
        ratio = norm_next / norm_now
        return residual, residual + ratio * direction, norm_next, norm_next + ratio * ratio * length, result

    def finish(lanes, state, square):
        _, direction, norm_now, length, result = state
        out_ref[:, lanes] = result + norm_now / (square + length) * direction[:own]

    def begin(residual):
        norm_now = total(residual * residual)
        return residual, residual, norm_now, norm_now, jnp.zeros((own, residual.shape[1]), jnp.float32)

    width = math.gcd(users, 256)
    groups = [slice(at, at + width) for at in range(0, users, width)]
    states = [begin(target(lanes)) for lanes in groups]
    for _ in range(ITERS - 1):
        images = [back(lanes, look(lanes, state[1]), state[1]) for lanes, state in zip(groups, states)]
        states = [advance(state, image) for state, image in zip(states, images)]
    for lanes, state in zip(groups, states):
        finish(lanes, state, square(lanes, state[1]))


def dense_shards(item_factors, send_list, obs_slot, obs_weight, rating, counts):
    own, items = item_factors.shape
    row_count = lax.axis_size("rows")
    col_count = lax.axis_size("cols")
    slots = send_list.shape[2]
    obs, users = obs_slot.shape
    positions = row_count * slots
    factor_count = own * col_count
    vmem = pl.BlockSpec(memory_space=pltpu.VMEM)
    hbm = pl.BlockSpec(memory_space=pltpu.HBM)

    def in_hbm(array):
        return pltpu.with_memory_space_constraint(array, pltpu.HBM)

    chunk_rows = 8 * row_count * col_count
    outgoing = pl.pallas_call(
        functools.partial(pick_kernel, col_count),
        out_shape=jax.ShapeDtypeStruct((chunk_rows, 128), jnp.bfloat16),
        in_specs=[hbm] * 2,
        out_specs=hbm,
        scratch_shapes=[
            pltpu.VMEM(item_factors.shape, item_factors.dtype),
            pltpu.VMEM(send_list.shape, send_list.dtype),
            pltpu.VMEM((chunk_rows, 128), jnp.bfloat16),
            pltpu.SemaphoreType.DMA((5,)),
            pltpu.SemaphoreType.DMA((2 * positions // 128,)),
        ],
        compiler_params=pltpu.CompilerParams(vmem_limit_bytes=4 << 20),
        name="pick",
    )(*map(in_hbm, (item_factors, send_list)))
    arrived = lax.all_to_all(outgoing, ("rows", "cols"), split_axis=0, concat_axis=0, tiled=True)
    counts = counts.reshape(1, users)
    weight, value = pl.pallas_call(
        spread_kernel,
        out_shape=(
            pltpu.VMEM((positions, users), jnp.float32),
            pltpu.VMEM((2 * positions, users), jnp.bfloat16),
        ),
        in_specs=[hbm] * 4,
        out_specs=[vmem] * 2,
        scratch_shapes=[
            pltpu.VMEM((obs, users), jnp.int32),
            pltpu.VMEM((obs, users), jnp.float32),
            pltpu.VMEM((obs, users), jnp.float32),
            pltpu.VMEM((1, users), jnp.int32),
            pltpu.VMEM((32 * obs, 128), jnp.int8),
            pltpu.VMEM((positions, users), jnp.int8),
            pltpu.SemaphoreType.DMA((4,)),
        ],
        compiler_params=pltpu.CompilerParams(vmem_limit_bytes=8 << 20),
        cost_estimate=pl.CostEstimate(
            flops=3 * obs * positions * users, bytes_accessed=(12 * obs + 8 * positions) * users, transcendentals=0
        ),
        name="spread",
    )(*map(in_hbm, (obs_slot, obs_weight, rating, counts)))
    return pl.pallas_call(
        functools.partial(solve_kernel, slots=slots, col_count=col_count),
        out_shape=jax.ShapeDtypeStruct((own, users), jnp.float32),
        in_specs=[vmem] * 3,
        out_specs=vmem,
        scratch_shapes=[
            pltpu.VMEM((chunk_rows, 128), jnp.float32),
            pltpu.VMEM((positions, 2 * factor_count), jnp.bfloat16),
            pltpu.VMEM((factor_count, 2 * positions), jnp.bfloat16),
            pltpu.VMEM((factor_count, users), jnp.float32),
        ],
        compiler_params=pltpu.CompilerParams(vmem_limit_bytes=32 << 20),
        name="solve",
    )(arrived, weight, value)


def shards(item_factors, send_list, obs_slot, obs_weight, rating, counts):
    positions = lax.axis_size("rows") * send_list.shape[2]
    obs = obs_slot.shape[0]
    own = item_factors.shape[0]
    packs = own % 8 == 0 and own // 8 * send_list.shape[2] <= 128
    dense = packs and positions <= 256 and positions % 128 == 0 and 128 % send_list.shape[2] == 0 and obs <= 64 and obs & (obs - 1) == 0
    work = dense_shards if dense else sparse_shards
    return work(item_factors, send_list, obs_slot, obs_weight, rating, counts)


def solution(mesh):
    placed = (
        P("cols", "rows"),
        P("rows", None, None),
        P(None, "rows"),
        P(None, "rows"),
        P(None, "rows"),
        P("rows"),
    )
    return jax.shard_map(
        shards, mesh=mesh, in_specs=placed, out_specs=P("cols", "rows"), check_vma=False
    )
```

```python
import functools
import math

import jax
import jax.numpy as jnp
from jax import lax
from jax.experimental import pallas as pl
from jax.experimental.pallas import tpu as pltpu
from jax.sharding import PartitionSpec as P

ITERS = 4


ridge_scale = 0.05


def update(tiles, weighted, ridge, direction, along, length_sq, norm_now, solution, residual):
    scaled = weighted * along
    image = jnp.sum(tiles * scaled[None], axis=1) + ridge * direction
    curvature = jnp.sum(scaled * along, axis=0) + ridge * length_sq
    step_size = norm_now / curvature
    return (solution + step_size * direction, residual - step_size * image)


def squared_norm(values):
    partial_sum = jnp.sum(values * values, axis=0)
    return lax.psum(partial_sum, "cols")


def conjugate_plain(tiles, weighted, rating, ridge):
    target = jnp.sum(tiles * (weighted * rating)[None], axis=1)
    solution = jnp.zeros_like(target)
    residual = target
    direction = target
    norm_now = squared_norm(target)
    for iteration in range(ITERS):
        along_part = jnp.sum(tiles * direction[:, None, :], axis=0)
        length_part = jnp.sum(direction * direction, axis=0)
        along, length_sq = lax.psum((along_part, length_part), "cols")
        solution, residual = update(
            tiles, weighted, ridge, direction, along, length_sq, norm_now, solution, residual
        )
        if iteration + 1 < ITERS:
            norm_next = squared_norm(residual)
            direction = residual + norm_next / norm_now * direction
            norm_now = norm_next
    return solution


def sparse_shards(item_factors, send_list, obs_slot, obs_weight, rating, counts):
    columns = item_factors.shape[0]
    row_count = lax.axis_size("rows")
    slot_count = send_list.shape[2]
    outgoing = jnp.take(item_factors, send_list.reshape(-1), axis=1).reshape(
        columns, row_count, slot_count
    )
    arrived = lax.all_to_all(outgoing, "rows", split_axis=1, concat_axis=1, tiled=True).reshape(
        columns, row_count * slot_count
    )
    tiles = jnp.take(arrived, obs_slot, axis=1)
    present = jnp.arange(obs_slot.shape[0], dtype=jnp.int32)[:, None] < counts[None, :]
    weighted = jnp.where(present, obs_weight, jnp.float32(0.0))
    ridge = ridge_scale * counts.astype(jnp.float32)
    return conjugate_plain(tiles, weighted, rating, ridge)


def pieces_of(values, count):
    pieces = []
    for _ in range(count):
        piece = values.astype(jnp.bfloat16)
        pieces.append(piece)
        values = values - piece.astype(jnp.float32)
    return jnp.concatenate(pieces, axis=0)


def swap_blocks(parts, width, wanted):
    count = 128 // width
    block = lax.broadcasted_iota(jnp.int32, (8, 128), 1) // width
    turned = []
    for shift in range(count):
        line = None
        for at in range(count):
            source = (at + shift) % count
            if source < len(parts):
                line = parts[source] if line is None else jnp.where(block == at, parts[source], line)
        turned.append(pltpu.roll(line, width * shift, 1) if shift else line)
    results = []
    for a in range(wanted):
        result = turned[-a % count]
        for b in range(1, len(parts)):
            result = jnp.where(block == b, turned[(b - a) % count], result)
        results.append(result)
    return results


def pick_kernel(col_count, factors_ref, list_ref, out_ref, factors, wanted, ready, arrived, left):
    factor_count, items = factors.shape
    _, row_count, slots = wanted.shape
    list_copy = pltpu.make_async_copy(list_ref, wanted, arrived.at[0])
    quarter = items // 4
    factors_copies = []
    for part in range(4):
        lanes = pl.ds(quarter * part, quarter)
        factors_copies.append(
            pltpu.make_async_copy(factors_ref.at[:, lanes], factors.at[:, lanes], arrived.at[1 + part])
        )
    list_copy.start()
    for copy in factors_copies:
        copy.start()
    within = lax.broadcasted_iota(jnp.int32, (128, row_count * slots), 0)
    list_copy.wait()
    item = jnp.concatenate([wanted[0, d : d + 1, :] for d in range(row_count)], axis=1)
    chosen = jnp.where(within == (item & 127), jnp.float32(1), jnp.float32(0)).astype(jnp.bfloat16)
    for copy in factors_copies:
        copy.wait()
    groups = items // 128
    stacked = jnp.concatenate([factors[:, 128 * g : 128 * (g + 1)] for g in range(groups)], axis=0)
    found = jnp.dot(stacked, chosen, preferred_element_type=jnp.float32)
    picked = found[:factor_count]
    for g in range(1, groups):
        picked = jnp.where(item >> 7 == g, found[factor_count * g : factor_count * (g + 1)], picked)
    per_tile = 128 // slots
    chunk_rows = 8 * col_count
    copies = []
    for first in range(0, row_count, per_tile):
        lines = picked[:, first * slots : first * slots + 128]
        parts = [lines[8 * i : 8 * i + 8] for i in range(factor_count // 8)]
        for d, chunk in enumerate(swap_blocks(parts, slots, per_tile), first):
            chunk = jnp.concatenate([chunk] * col_count, axis=0).astype(jnp.bfloat16)
            ready[chunk_rows * d : chunk_rows * (d + 1), :] = chunk
        half = chunk_rows * per_tile // 2
        for start in (chunk_rows * first, chunk_rows * first + half):
            part = pl.ds(start, half)
            copy = pltpu.make_async_copy(ready.at[part], out_ref.at[part], left.at[len(copies)])
            copy.start()
            copies.append(copy)
    for copy in copies:
        copy.wait()


def spread_kernel(
    slot_hbm, weight_hbm, rating_hbm, counts_hbm, w_ref, b_ref,
    slot_ref, weight_ref, rating_ref, counts_ref, wanted, named, arrived
):
    obs, users = slot_ref.shape
    positions = w_ref.shape[0]
    groups = obs // 8
    levels = groups.bit_length() - 1
    rows = 32
    copies = [
        pltpu.make_async_copy(source, target, arrived.at[at])
        for at, (source, target) in enumerate(
            ((slot_hbm, slot_ref), (weight_hbm, weight_ref), (rating_hbm, rating_ref), (counts_hbm, counts_ref))
        )
    ]
    for copy in copies:
        copy.start()
    copies[0].wait()

    @pl.loop(0, users // 128)
    def _(tile):
        lanes = pl.ds(pl.multiple_of(tile * 128, 128), 128)
        row = lax.broadcasted_iota(jnp.int32, (rows, 128), 0)
        for o in range(obs):
            position = jnp.broadcast_to(slot_ref[o : o + 1, lanes], (rows, 128))
            wanted[rows * o : rows * (o + 1), :] = (position - 128).astype(jnp.int8)
        places = [(row + (rows * k - 128)).astype(jnp.int8) for k in range(positions // rows)]
        found = [jnp.full((rows, 128), obs, jnp.int8) for _ in places]
        for o in reversed(range(obs)):
            position = wanted[rows * o : rows * (o + 1), :]
            found = [jnp.where(position == place, jnp.int8(o), last) for place, last in zip(places, found)]
        for k, slot in enumerate(found):
            named[rows * k : rows * (k + 1), lanes] = slot

    for copy in copies[1:]:
        copy.wait()

    @pl.loop(0, users // 128)
    def _(tile):
        lanes = pl.ds(pl.multiple_of(tile * 128, 128), 128)
        live = counts_ref[:, lanes]
        scale = 1.0 / (ridge_scale * live.astype(jnp.float32))
        weights = [weight_ref[8 * g : 8 * g + 8, lanes] for g in range(groups)]
        ratings = [rating_ref[8 * g : 8 * g + 8, lanes] for g in range(groups)]
        for k in range(positions // rows):
            slots = named[rows * k : rows * (k + 1), lanes].astype(jnp.int32)
            values = []
            for at in range(0, rows, 8):
                slot = slots[at : at + 8]
                within = slot & 7
                bits = [(slot & (8 << level)) != 0 for level in range(levels)]

                def fetch(blocks):
                    picked = [jnp.take_along_axis(block, within, axis=0) for block in blocks]
                    for bit in bits:
                        picked = [jnp.where(bit, picked[e + 1], picked[e]) for e in range(0, len(picked), 2)]
                    return picked[0]

                weight = jnp.where(slot < live, fetch(weights) * scale, 0.0)
                w_ref[rows * k + at : rows * k + at + 8, lanes] = weight
                values.append(weight * fetch(ratings))
            values = jnp.concatenate(values, axis=0)
            for piece in range(2):
                part = values.astype(jnp.bfloat16)
                at = rows * k // 128 * 256 + 128 * piece + rows * k % 128
                b_ref[at : at + rows, lanes] = part
                values = values - part.astype(jnp.float32)


def solve_kernel(arrived_ref, w_ref, b_ref, out_ref, unpacked, twice_t, twice, image_ref, slots, col_count):
    own, users = out_ref.shape
    positions = w_ref.shape[0]
    factor_count = own * col_count
    row_count = positions // slots

    unpacked[...] = arrived_ref[...].astype(jnp.float32)
    me = lax.axis_index("cols")
    per_tile = 128 // slots
    for j in range(col_count):
        source = lax.rem(me + j, col_count)
        chunks = [unpacked[pl.ds(8 * (s * col_count + source), 8), :] for s in range(row_count)]
        tiles = [
            jnp.concatenate(swap_blocks(chunks[first : first + per_tile], slots, own // 8), axis=0)
            for first in range(0, row_count, per_tile)
        ]
        block = jnp.concatenate(tiles, axis=1)
        for part in range(positions // 128):
            for copy in range(2):
                at = 256 * part + 128 * copy
                twice[own * j : own * (j + 1), at : at + 128] = block[:, 128 * part : 128 * part + 128].astype(jnp.bfloat16)
    for part in range(positions // 128):
        columns = twice[:, 256 * part : 256 * part + 128].astype(jnp.float32)
        columns_t = jnp.transpose(columns).astype(jnp.bfloat16)
        for copy in range(2):
            twice_t[128 * part : 128 * part + 128, factor_count * copy : factor_count * (copy + 1)] = columns_t

    def dot(left, right):
        return jnp.dot(left, right, preferred_element_type=jnp.float32)

    def total(values):
        while values.shape[0] > 8:
            half = values.shape[0] // 2
            values = values[:half] + values[half:]
        return jnp.sum(values, axis=0, keepdims=True)

    def target(lanes):
        parts = [slice(at, at + 256) for at in range(0, 2 * positions, 256)]
        return sum(dot(twice[:, part], b_ref[part, lanes]) for part in parts)

    def look(lanes, direction):
        along = dot(twice_t[...], pieces_of(direction, 2))
        parts = [slice(at, at + 128) for at in range(0, positions, 128)]
        return [(along[part], w_ref[part, lanes] * along[part]) for part in parts]

    def square(lanes, direction):
        pieces = pieces_of(direction, 2)
        parts = [slice(at, at + 128) for at in range(0, positions, 128)]
        views = [(dot(twice_t[part], pieces), w_ref[part, lanes]) for part in parts]
        return sum(total(weight * along * along) for along, weight in views)

    def back(lanes, views, direction):
        pieces = jnp.concatenate([pieces_of(scaled, 2) for _, scaled in views], axis=0)
        image_ref[:, lanes] = dot(twice[...], pieces)
        return image_ref[:, lanes] + direction

    def advance(state, image):
        residual, direction, norm_now, length, result = state
        step_size = norm_now / total(image * direction)
        result = result + step_size * direction[:own]
        residual = residual - step_size * image
        norm_next = total(residual * residual)
        ratio = norm_next / norm_now
        return residual, residual + ratio * direction, norm_next, norm_next + ratio * ratio * length, result

    def finish(lanes, state, square):
        _, direction, norm_now, length, result = state
        out_ref[:, lanes] = result + norm_now / (square + length) * direction[:own]

    def begin(residual):
        norm_now = total(residual * residual)
        return residual, residual, norm_now, norm_now, jnp.zeros((own, residual.shape[1]), jnp.float32)

    width = math.gcd(users, 256)
    groups = [slice(at, at + width) for at in range(0, users, width)]
    states = [begin(target(lanes)) for lanes in groups]
    for _ in range(ITERS - 1):
        images = [back(lanes, look(lanes, state[1]), state[1]) for lanes, state in zip(groups, states)]
        states = [advance(state, image) for state, image in zip(states, images)]
    for lanes, state in zip(groups, states):
        finish(lanes, state, square(lanes, state[1]))


def dense_shards(item_factors, send_list, obs_slot, obs_weight, rating, counts):
    own, items = item_factors.shape
    row_count = lax.axis_size("rows")
    col_count = lax.axis_size("cols")
    slots = send_list.shape[2]
    obs, users = obs_slot.shape
    positions = row_count * slots
    factor_count = own * col_count
    vmem = pl.BlockSpec(memory_space=pltpu.VMEM)
    hbm = pl.BlockSpec(memory_space=pltpu.HBM)

    def in_hbm(array):
        return pltpu.with_memory_space_constraint(array, pltpu.HBM)

    chunk_rows = 8 * row_count * col_count
    outgoing = pl.pallas_call(
        functools.partial(pick_kernel, col_count),
        out_shape=jax.ShapeDtypeStruct((chunk_rows, 128), jnp.bfloat16),
        in_specs=[hbm] * 2,
        out_specs=hbm,
        scratch_shapes=[
            pltpu.VMEM(item_factors.shape, item_factors.dtype),
            pltpu.VMEM(send_list.shape, send_list.dtype),
            pltpu.VMEM((chunk_rows, 128), jnp.bfloat16),
            pltpu.SemaphoreType.DMA((5,)),
            pltpu.SemaphoreType.DMA((2 * positions // 128,)),
        ],
        compiler_params=pltpu.CompilerParams(vmem_limit_bytes=4 << 20),
        name="pick",
    )(*map(in_hbm, (item_factors, send_list)))
    arrived = lax.all_to_all(outgoing, ("rows", "cols"), split_axis=0, concat_axis=0, tiled=True)
    counts = counts.reshape(1, users)
    weight, value = pl.pallas_call(
        spread_kernel,
        out_shape=(
            pltpu.VMEM((positions, users), jnp.float32),
            pltpu.VMEM((2 * positions, users), jnp.bfloat16),
        ),
        in_specs=[hbm] * 4,
        out_specs=[vmem] * 2,
        scratch_shapes=[
            pltpu.VMEM((obs, users), jnp.int32),
            pltpu.VMEM((obs, users), jnp.float32),
            pltpu.VMEM((obs, users), jnp.float32),
            pltpu.VMEM((1, users), jnp.int32),
            pltpu.VMEM((32 * obs, 128), jnp.int8),
            pltpu.VMEM((positions, users), jnp.int8),
            pltpu.SemaphoreType.DMA((4,)),
        ],
        compiler_params=pltpu.CompilerParams(vmem_limit_bytes=8 << 20),
        cost_estimate=pl.CostEstimate(
            flops=3 * obs * positions * users, bytes_accessed=(12 * obs + 8 * positions) * users, transcendentals=0
        ),
        name="spread",
    )(*map(in_hbm, (obs_slot, obs_weight, rating, counts)))
    return pl.pallas_call(
        functools.partial(solve_kernel, slots=slots, col_count=col_count),
        out_shape=jax.ShapeDtypeStruct((own, users), jnp.float32),
        in_specs=[vmem] * 3,
        out_specs=vmem,
        scratch_shapes=[
            pltpu.VMEM((chunk_rows, 128), jnp.float32),
            pltpu.VMEM((positions, 2 * factor_count), jnp.bfloat16),
            pltpu.VMEM((factor_count, 2 * positions), jnp.bfloat16),
            pltpu.VMEM((factor_count, users), jnp.float32),
        ],
        compiler_params=pltpu.CompilerParams(vmem_limit_bytes=32 << 20),
        name="solve",
    )(arrived, weight, value)


def shards(item_factors, send_list, obs_slot, obs_weight, rating, counts):
    positions = lax.axis_size("rows") * send_list.shape[2]
    obs = obs_slot.shape[0]
    own = item_factors.shape[0]
    packs = own % 8 == 0 and own // 8 * send_list.shape[2] <= 128
    dense = packs and positions <= 256 and positions % 128 == 0 and 128 % send_list.shape[2] == 0 and obs <= 64 and obs & (obs - 1) == 0
    work = dense_shards if dense else sparse_shards
    return work(item_factors, send_list, obs_slot, obs_weight, rating, counts)


def solution(mesh):
    placed = (
        P("cols", "rows"),
        P("rows", None, None),
        P(None, "rows"),
        P(None, "rows"),
        P(None, "rows"),
        P("rows"),
    )
    return jax.shard_map(
        shards, mesh=mesh, in_specs=placed, out_specs=P("cols", "rows"), check_vma=False
    )
```
